768 devices in a mesh: rep: 96 (over x, z, core), shard: 8 (over y).
Axes of the slice: x: 4, y: 8, z: 12, core: 2. Of those that a mesh axis runs over, the one named last changes fastest.
Arguments:
- accumulated: bfloat16 [96, 3072, 3072], P('rep', None, 'shard'), may hold values from -12 to 12
- prior_right: bfloat16 [3072, 64], P('shard'), may hold values from -0.109375 to 0.109375
Outputs:
- update: bfloat16 [3072, 3072], P(None, 'shard')
- carried_error: bfloat16 [96, 3072, 3072], P('rep', None, 'shard')
The draws below stay inside these ranges and needn't reach their ends.
All inputs are finite; a program needn't handle non-finite values.
Results may differ from the reference program's by a relative error of at most 0.0042.
Values sent between devices are 32-bit elements; how exact they have to be, the bound alone decides.
A program may use at most 32 MiB of HBM per device.

```python
import jax
import jax.numpy as jnp
from jax import lax

ROWS = 3072
COLS = 3072
RANK = 64
REPS = 96


def draw_accumulated(key, part):
    key = jax.random.fold_in(key, 11)
    first, second, third, fourth = jax.random.split(key, 4)
    common = jax.random.normal(first, (ROWS, COLS), jnp.float32)
    noise = jax.random.normal(second, (REPS, ROWS, COLS), jnp.float32)
    row_scale = jnp.exp(jax.random.uniform(third, (ROWS,), jnp.float32, -1.15, 1.15))
    col_scale = jnp.exp(jax.random.uniform(fourth, (COLS,), jnp.float32, -0.7, 0.7))
    steps = jnp.arange(REPS, dtype=jnp.float32) / max(REPS - 1, 1)
    rep_scale = 0.5 + steps
    values = (0.6 * common[None] + rep_scale[:, None, None] * noise) * row_scale[None, :, None] * col_scale[None, None, :] * 0.5
    return jnp.clip(values, -12.0, 12.0).astype(jnp.bfloat16)


def steps_of(key, extent, cuts, least, top_value):
    level = 1.0
    for position, blocks in cuts:
        heights = jax.random.uniform(jax.random.fold_in(jax.random.fold_in(key, 6), position), (blocks,), jnp.float32, least / len(cuts), top_value / len(cuts))
        level = level * jnp.repeat(jnp.exp(heights), extent[position] // blocks).reshape((-1,) + (1,) * (len(extent) - 1 - position))
    return level


def bell_draw(rng, shape, scale, bound, pieces=(), kind=jnp.bfloat16):
    loudness = steps_of(rng, shape, pieces, -0.22, 0.18) if pieces else 1.0
    array = jax.random.normal(rng, shape, jnp.float32) * scale * loudness
    return jnp.minimum(jnp.maximum(array, -bound), bound).astype(kind)


def setup_inputs(seed: int = 0) -> dict:
    key_list = jax.random.split(jax.random.key(seed), 3)
    return {
        "accumulated": draw_accumulated(jax.random.fold_in(key_list[2], 71), 0),
        "prior_right": bell_draw(key_list[1], (COLS, RANK), COLS ** -0.5, 0.109375, ((0, 8),)),
    }


def orthonormal(left):
    gram = jnp.dot(left.T.astype(jnp.float32), left.astype(jnp.float32), precision=lax.Precision.HIGHEST, preferred_element_type=jnp.float32)
    factor = jnp.linalg.cholesky(gram)
    return jax.scipy.linalg.solve_triangular(factor, left.T, lower=True).T

def reference(accumulated, prior_right):

    def add_left(total, block):
        return (total + jnp.dot(block.astype(jnp.float32), prior_right.astype(jnp.float32), preferred_element_type=jnp.float32), None)
    left, _ = lax.scan(add_left, jnp.zeros((ROWS, RANK), jnp.float32), accumulated)
    basis = orthonormal(left)
    basis_low = basis.astype(jnp.bfloat16)

    def add_right(total, block):
        term = jnp.einsum('nm,nr->mr', block.astype(jnp.float32), basis_low.astype(jnp.float32), preferred_element_type=jnp.float32)
        return (total + term, None)
    right, _ = lax.scan(add_right, jnp.zeros((COLS, RANK), jnp.float32), accumulated)
    right = right / REPS
    decoded = jnp.dot(basis.astype(jnp.float32), right.T.astype(jnp.float32), precision=lax.Precision.HIGHEST, preferred_element_type=jnp.float32)

    def residue(block):
        return (block.astype(jnp.float32) - decoded).astype(jnp.bfloat16)
    carried_error = lax.map(residue, accumulated)
    return (decoded.astype(jnp.bfloat16), carried_error)
```

```python
import functools

import jax
import jax.numpy as jnp
from jax import lax
from jax.experimental import pallas as pl
from jax.experimental.pallas import tpu as pltpu
from jax.sharding import PartitionSpec as P

MESH = pl.DeviceIdType.MESH
NX, NY, NZ, NC = 4, 8, 12, 2
REPS = NX * NZ * NC
RANK = 64
GROUP = RANK // (NX * NC)
HALF = RANK // NC
BLOCK = 384
COLS = 384
X_FAR = (2, 1, 3)
Y_FAR = (4, 3, 5, 2, 6, 1, 7)
Y_NEAR = (0, 1, 7, 2, 6, 3, 5, 4)
Z_FAR = (6, 5, 7, 4, 8, 3, 9, 2, 10, 1, 11)
XC_FAR = ((2, 1), (2, 0), (1, 1), (3, 1), (1, 0), (3, 0), (0, 1))
F32, BF16 = jnp.float32, jnp.bfloat16
NT = (((1,), (1,)), ((), ()))


def split3(value):
    high = value.astype(BF16)
    rest = value - high.astype(F32)
    middle = rest.astype(BF16)
    low = (rest - middle.astype(F32)).astype(BF16)
    return high, middle, low


def eliminate(tiles, first, last):
    tiles = list(tiles)
    rows = lax.broadcasted_iota(jnp.int32, (8, 1), 0)
    for k in range(first, last):
        own, at = divmod(k, 8)
        row = tiles[own][at : at + 1, :]
        scaled = row * (1.0 / row[:, k : k + 1])
        for i in range(own, 8):
            column = tiles[i][:, k : k + 1]
            if i == own:
                column = jnp.where(rows > at, column, 0.0)
            tiles[i] = tiles[i] - column * scaled
    return tiles


def exchange_kernel(
    pt_ref, a_ref, bk_ref, rk_ref,
    a_v, part, sib, half, xr, yb, yr, zr, left, racc, gacc, rpart, rr, zr2, rt, bk_v, w_v,
    a_sem, cs, cr, xs, xrs, ys, yrs, zs, zrs, ays, ayr, axs, axr, acs, acr,
    rs, rrs, z2s, z2r, qs, qr, bk_sem,
):
    rep, y = lax.axis_index("rep"), lax.axis_index("shard")
    x, z, c = rep // (NZ * NC), (rep // NC) % NZ, rep % NC

    def device(dx=0, dy=0, dz=0, dc=0):
        return (
            (((x + dx) % NX) * NZ + (z + dz) % NZ) * NC + (c + dc) % NC,
            (y + dy) % NY,
        )

    def send(src, dst, send_sem, recv_sem, where):
        return pltpu.make_async_remote_copy(
            src_ref=src, dst_ref=dst, send_sem=send_sem, recv_sem=recv_sem,
            device_id=where, device_id_type=MESH,
        )

    sent = []

    def start(copy):
        copy.start()
        sent.append(copy)

    barrier = pltpu.get_barrier_semaphore()
    partners = (
        [device(dz=o) for o in Z_FAR]
        + [device(dy=d) for d in Y_FAR]
        + [device(dx=ox, dc=oc) for ox, oc in XC_FAR]
    )
    for partner in partners:
        pl.semaphore_signal(barrier, inc=1, device_id=partner, device_id_type=MESH)

    rs_order = Y_FAR + (0,)
    a_copies = {}
    for d in rs_order:
        b = (y + d) % NY
        a_copies[d] = pltpu.make_async_copy(a_ref.at[b], a_v.at[b], a_sem.at[d])
        a_copies[d].start()

    group = c * NX + x
    mine = pl.ds(pl.multiple_of(group * GROUP, GROUP), GROUP)
    my_half = pl.ds(pl.multiple_of(c * HALF, HALF), HALF)
    its_half = pl.ds(pl.multiple_of((1 - c) * HALF, HALF), HALF)
    sibling = device(dc=1)

    def product(d):
        b = (y + d) % NY
        a_copies[d].wait()
        part[b] = lax.dot_general(pt_ref[...], a_v[b], NT, preferred_element_type=F32)

    def core_copy(d):
        b = (y + d) % NY
        return send(part.at[b, its_half], sib.at[b], cs.at[d], cr.at[d], sibling)

    def x_copy(i, d):
        o, b = X_FAR[i], (y + d) % NY
        rows = pl.ds(pl.multiple_of(((x + o) % NX) * GROUP, GROUP), GROUP)
        return send(half.at[b, rows], xr.at[i, b], xs.at[i, d], xrs.at[i, d], device(dx=o))

    def core_sum(d):
        b = (y + d) % NY
        core_copy(d).wait_recv()
        half[b] = part[b, my_half] + sib[b]
        for i in range(3):
            start(x_copy(i, d))

    product(rs_order[0])
    product(rs_order[1])
    pl.semaphore_wait(barrier, len(partners))
    start(core_copy(rs_order[0]))
    start(core_copy(rs_order[1]))
    for t in range(2, 8):
        product(rs_order[t])
        start(core_copy(rs_order[t]))
        core_sum(rs_order[t - 2])
    core_sum(rs_order[6])
    core_sum(rs_order[7])

    my_x = pl.ds(pl.multiple_of(x * GROUP, GROUP), GROUP)

    def y_copy(d):
        return send(yb.at[d], yr.at[d], ys.at[d], yrs.at[d], device(dy=d))

    for d in rs_order:
        b = (y + d) % NY
        for i in range(3):
            x_copy(i, d).wait_recv()
        yb[d] = half[b, my_x] + xr[0, b] + xr[1, b] + xr[2, b]
        if d:
            start(y_copy(d))
    total = yb[0]
    for d in (1, 7, 2, 6, 3, 5, 4):
        y_copy(d).wait_recv()
        total = total + yr[d]

    def z_copy(ref, send_sem, recv_sem, o):
        return send(ref.at[z], ref.at[z], send_sem.at[o], recv_sem.at[o], device(dz=o))

    def z_wait(ref, send_sem, recv_sem, o):
        at = ref.at[(z + NZ - o) % NZ]
        send(at, at, send_sem.at[o], recv_sem.at[o], device(dz=o)).wait_recv()

    def z_sum(ref):
        value = ref[0]
        for i in range(1, NZ):
            value = value + ref[i]
        return value

    zr[z] = total
    for o in Z_FAR:
        start(z_copy(zr, zs, zrs, o))
    for o in reversed(Z_FAR):
        z_wait(zr, zs, zrs, o)
    left[y, mine] = z_sum(zr)

    def ay_copy(d, at):
        ref = left.at[at, mine]
        return send(ref, ref, ays.at[d], ayr.at[d], device(dy=d))

    def ax_copy(i, d):
        ref = left.at[(y + NY - d) % NY, mine]
        return send(ref, ref, axs.at[i, d], axr.at[i, d], device(dx=X_FAR[i]))

    def ax_wait(i, d):
        theirs = c * NX + (x + NX - X_FAR[i]) % NX
        rows = pl.ds(pl.multiple_of(theirs * GROUP, GROUP), GROUP)
        ref = left.at[(y + NY - d) % NY, rows]
        send(ref, ref, axs.at[i, d], axr.at[i, d], device(dx=X_FAR[i])).wait_recv()

    def ac_copy(d):
        ref = left.at[(y + NY - d) % NY, my_half]
        return send(ref, ref, acs.at[d], acr.at[d], sibling)

    def ac_wait(d):
        ref = left.at[(y + NY - d) % NY, its_half]
        send(ref, ref, acs.at[d], acr.at[d], sibling).wait_recv()

    for d in Y_FAR:
        start(ay_copy(d, y))
    for d in Y_NEAR:
        if d:
            ay_copy(d, (y + NY - d) % NY).wait_recv()
        for i in range(3):
            start(ax_copy(i, d))

    def contract(d):
        b = (y + NY - d) % NY
        ac_wait(d)
        pieces = jnp.concatenate(split3(left[b]), axis=0)
        r = jnp.dot(pieces, a_v[b], preferred_element_type=F32)
        g = lax.dot_general(pieces, pieces, NT, preferred_element_type=F32)
        if d:
            racc[...] += r
            gacc[...] += g
        else:
            racc[...] = r
            gacc[...] = g

    for t, d in enumerate(Y_NEAR):
        for i in range(3):
            ax_wait(i, d)
        start(ac_copy(d))
        if t >= 2:
            contract(Y_NEAR[t - 2])
    contract(Y_NEAR[6])
    contract(Y_NEAR[7])

    rpart[...] = racc[0:64] + racc[64:128] + racc[128:192]

    def r_copy(i):
        ox, oc = XC_FAR[i]
        theirs = ((c + oc) % NC) * NX + (x + ox) % NX
        rows = pl.ds(pl.multiple_of(theirs * GROUP, GROUP), GROUP)
        return send(rpart.at[rows], rr.at[i], rs.at[i], rrs.at[i], device(dx=ox, dc=oc))

    for i in range(7):
        start(r_copy(i))

    one = gacc[0:64, 0:64]
    cross = gacc[0:64, 64:128] + gacc[64:128, 0:64]
    small = gacc[64:128, 64:128] + gacc[0:64, 128:192] + gacc[128:192, 0:64]
    gram = one + (cross + small)
    at_row = lax.broadcasted_iota(jnp.int32, (64, 64), 0)
    at_col = lax.broadcasted_iota(jnp.int32, (64, 64), 1)
    diagonal = at_row == at_col
    both = jnp.concatenate([gram, jnp.where(diagonal, 1.0, 0.0).astype(F32)], axis=1)
    tiles = eliminate([both[8 * i : 8 * i + 8] for i in range(8)], 0, 24)

    total = rpart[mine]
    for i in reversed(range(7)):
        r_copy(i).wait_recv()
        total = total + rr[i]
    zr2[z] = total
    for o in Z_FAR:
        start(z_copy(zr2, z2s, z2r, o))

    both = jnp.concatenate(eliminate(tiles, 24, 64), axis=0)
    scale = jnp.sum(jnp.where(diagonal, both[:, 0:64], 0.0), axis=1, keepdims=True)
    w_v[...] = both[:, 64:128] * (1.0 / jnp.sqrt(scale))

    for o in reversed(Z_FAR):
        z_wait(zr2, z2s, z2r, o)
    rt[mine] = z_sum(zr2)

    def q_copy(i):
        ox, oc = XC_FAR[i]
        ref = rt.at[mine]
        return send(ref, ref, qs.at[i], qr.at[i], device(dx=ox, dc=oc))

    def q_wait(i):
        ox, oc = XC_FAR[i]
        theirs = ((c + NC - oc) % NC) * NX + (x + NX - ox) % NX
        rows = pl.ds(pl.multiple_of(theirs * GROUP, GROUP), GROUP)
        ref = rt.at[rows]
        send(ref, ref, qs.at[i], qr.at[i], device(dx=ox, dc=oc)).wait_recv()

    for i in range(7):
        start(q_copy(i))

    for b in range(NY):
        basis_t = jnp.dot(
            w_v[...], left[b], precision=lax.Precision.HIGHEST, preferred_element_type=F32
        )
        high = basis_t.astype(BF16).astype(F32)
        low = basis_t - high
        packed = jnp.concatenate([high, high, low, low], axis=0)
        bk_v[b * BLOCK : (b + 1) * BLOCK] = packed.T.astype(BF16)
    out = pltpu.make_async_copy(bk_v, bk_ref, bk_sem)
    out.start()

    for i in reversed(range(7)):
        q_wait(i)
    right_t = jnp.dot(
        w_v[...], rt[...], precision=lax.Precision.HIGHEST, preferred_element_type=F32
    ) * (1.0 / REPS)
    high = right_t.astype(BF16)
    low = (right_t - high.astype(F32)).astype(BF16)
    rk_ref[...] = jnp.concatenate([high, low, high, low], axis=0)
    out.wait()
    for copy in sent:
        copy.wait_send()


def exchange(prior_t, blocks):
    dma = pltpu.SemaphoreType.DMA
    vmem = pltpu.VMEM
    return pl.pallas_call(
        exchange_kernel,
        out_shape=(
            jax.ShapeDtypeStruct((NY * BLOCK, 4 * RANK), BF16),
            jax.ShapeDtypeStruct((4 * RANK, COLS), BF16),
        ),
        in_specs=[
            pl.BlockSpec(memory_space=pltpu.VMEM),
            pl.BlockSpec(memory_space=pl.ANY),
        ],
        out_specs=(
            pl.BlockSpec(memory_space=pl.ANY),
            pl.BlockSpec(memory_space=pltpu.VMEM),
        ),
        scratch_shapes=[
            vmem((NY, BLOCK, COLS), BF16),
            vmem((NY, RANK, BLOCK), F32),
            vmem((NY, HALF, BLOCK), F32),
            vmem((NY, HALF, BLOCK), F32),
            vmem((3, NY, GROUP, BLOCK), F32),
            vmem((NY, GROUP, BLOCK), F32),
            vmem((NY, GROUP, BLOCK), F32),
            vmem((NZ, GROUP, BLOCK), F32),
            vmem((NY, RANK, BLOCK), F32),
            vmem((3 * RANK, COLS), F32),
            vmem((3 * RANK, 3 * RANK), F32),
            vmem((RANK, COLS), F32),
            vmem((7, GROUP, COLS), F32),
            vmem((NZ, GROUP, COLS), F32),
            vmem((RANK, COLS), F32),
            vmem((NY * BLOCK, 4 * RANK), BF16),
            vmem((RANK, RANK), F32),
            dma((8,)), dma((8,)), dma((8,)),
            dma((3, 8)), dma((3, 8)),
            dma((8,)), dma((8,)),
            dma((12,)), dma((12,)),
            dma((8,)), dma((8,)),
            dma((3, 8)), dma((3, 8)),
            dma((8,)), dma((8,)),
            dma((7,)), dma((7,)),
            dma((12,)), dma((12,)),
            dma((7,)), dma((7,)),
            dma,
        ],
        compiler_params=pltpu.CompilerParams(
            collective_id=0, has_side_effects=True, vmem_limit_bytes=32 * 2**20
        ),
        name="exchange",
    )(prior_t, blocks)


def finish_kernel(basis_ref, right_ref, a_ref, update_ref, error_ref):
    decoded = jnp.dot(basis_ref[...], right_ref[...], preferred_element_type=F32)
    update_ref[...] = decoded.astype(BF16)
    error_ref[...] = (a_ref[...].astype(F32) - decoded).astype(BF16)


def finish(basis, right, block):
    rows = 512
    tall = lambda width: pl.BlockSpec((rows, width), lambda i: (i, 0))
    shape = jax.ShapeDtypeStruct(block.shape, BF16)
    return pl.pallas_call(
        finish_kernel,
        grid=(block.shape[0] // rows,),
        out_shape=(shape, shape),
        in_specs=[
            tall(4 * RANK),
            pl.BlockSpec((4 * RANK, COLS), lambda i: (0, 0)),
            tall(COLS),
        ],
        out_specs=(tall(COLS), tall(COLS)),
        name="finish",
    )(basis, right, block)


def shards(accumulated, prior_right):
    block = accumulated[0]
    basis, right = exchange(prior_right.T, block.reshape(NY, BLOCK, COLS))
    update, error = finish(basis, right, block)
    return update, error[None]


def solution(mesh):
    placed = (P("rep", None, "shard"), P("shard", None))
    return jax.shard_map(
        shards,
        mesh=mesh,
        in_specs=placed,
        out_specs=(P(None, "shard"), P("rep", None, "shard")),
        check_vma=False,
    )
```

```python
import functools

import jax
import jax.numpy as jnp
from jax import lax
from jax.experimental import pallas as pl
from jax.experimental.pallas import tpu as pltpu
from jax.sharding import PartitionSpec as P

MESH = pl.DeviceIdType.MESH
NX, NY, NZ, NC = 4, 8, 12, 2
REPS = NX * NZ * NC
RANK = 64
GROUP = RANK // (NX * NC)
HALF = RANK // NC
BLOCK = 384
COLS = 384
X_FAR = (2, 1, 3)
Y_FAR = (4, 3, 5, 2, 6, 1, 7)
Y_NEAR = (0, 1, 7, 2, 6, 3, 5, 4)
LAST = 4
Z_FAR = (6, 5, 7, 4, 8, 3, 9, 2, 10, 1, 11)
XC_FAR = ((2, 1), (2, 0), (1, 1), (3, 1), (1, 0), (3, 0), (0, 1))
EXCHANGE_VMEM = int(49.95 * 2**20)
F32, BF16 = jnp.float32, jnp.bfloat16
NT = (((1,), (1,)), ((), ()))


def split3(value):
    high = value.astype(BF16)
    rest = value - high.astype(F32)
    middle = rest.astype(BF16)
    low = (rest - middle.astype(F32)).astype(BF16)
    return high, middle, low


def eliminate(tiles, first, last):
    tiles = list(tiles)
    rows = lax.broadcasted_iota(jnp.int32, (8, 1), 0)
    for k in range(first, last):
        own, at = divmod(k, 8)
        row = tiles[own][at : at + 1, :]
        scaled = row * (1.0 / row[:, k : k + 1])
        for i in range(own, 8):
            column = tiles[i][:, k : k + 1]
            if i == own:
                column = jnp.where(rows > at, column, 0.0)
            tiles[i] = tiles[i] - column * scaled
    return tiles


def exchange_kernel(
    pt_ref, a_ref, bk_ref, rk_ref, a_v,
    pt_v, part, sib, half, xr, yb, yr, zr, left, racc, gacc, rpart, rr, zr2, rt, both_v, w_v,
    pt_sem, a_sem, cs, cr, xs, xrs, ys, yrs, zs, zrs, ays, ayr, axs, axr, als, alr, acs, acr,
    rs, rrs, z2s, z2r, qs, qr,
):
    rep, y = lax.axis_index("rep"), lax.axis_index("shard")
    chip = lax.div(rep, NC)
    x, z, c = lax.div(chip, NZ), lax.rem(chip, NZ), lax.rem(rep, NC)

    @functools.cache
    def device(dx=0, dy=0, dz=0, dc=0):
        return (
            (lax.rem(x + dx, NX) * NZ + lax.rem(z + dz, NZ)) * NC + lax.rem(c + dc, NC),
            lax.rem(y + dy, NY),
        )

    @functools.cache
    def block_at(d):
        return lax.rem(y + NY + d, NY)

    @functools.cache
    def group_rows(dx, dc):
        theirs = lax.rem(c + NC + dc, NC) * NX + lax.rem(x + NX + dx, NX)
        return pl.ds(pl.multiple_of(theirs * GROUP, GROUP), GROUP)

    def send(src, dst, send_sem, recv_sem, where):
        return pltpu.make_async_remote_copy(
            src_ref=src, dst_ref=dst, send_sem=send_sem, recv_sem=recv_sem,
            device_id=where, device_id_type=MESH,
        )

    sent = []

    def start(copy):
        copy.start()
        sent.append(copy)

    def drain(count):
        for copy in sent[:count]:
            copy.wait_send()
        del sent[:count]

    barrier = pltpu.get_barrier_semaphore()
    partners = (
        [device(dz=o) for o in Z_FAR]
        + [device(dy=d) for d in Y_FAR]
        + [device(dx=ox, dc=oc) for ox, oc in XC_FAR]
    )
    for partner in partners:
        pl.semaphore_signal(barrier, inc=1, device_id=partner, device_id_type=MESH)

    pt_copy = pltpu.make_async_copy(pt_ref, pt_v, pt_sem)
    pt_copy.start()
    rs_order = Y_FAR + (0,)
    a_copies = {}
    for d in rs_order:
        b = block_at(d)
        a_copies[d] = pltpu.make_async_copy(a_ref.at[b], a_v.at[b], a_sem.at[d])
        a_copies[d].start()

    mine = group_rows(0, 0)
    my_half = pl.ds(pl.multiple_of(c * HALF, HALF), HALF)
    its_half = pl.ds(pl.multiple_of((1 - c) * HALF, HALF), HALF)
    sibling = device(dc=1)

    def product(d):
        b = block_at(d)
        a_copies[d].wait()
        part[b] = lax.dot_general(pt_v[...], a_v[b], NT, preferred_element_type=F32)

    def core_copy(d):
        b = block_at(d)
        return send(part.at[b, its_half], sib.at[b], cs.at[d], cr.at[d], sibling)

    def x_copy(i, d):
        o, b = X_FAR[i], block_at(d)
        rows = pl.ds(pl.multiple_of(lax.rem(x + o, NX) * GROUP, GROUP), GROUP)
        return send(half.at[b, rows], xr.at[i, b], xs.at[i, d], xrs.at[i, d], device(dx=o))

    def core_sum(d):
        b = block_at(d)
        core_copy(d).wait_recv()
        half[b] = part[b, my_half] + sib[b]
        for i in range(3):
            start(x_copy(i, d))

    pt_copy.wait()
    for d in rs_order:
        product(d)
    pl.semaphore_wait(barrier, len(partners))
    for d in rs_order:
        start(core_copy(d))
    for d in rs_order:
        core_sum(d)

    my_x = pl.ds(pl.multiple_of(x * GROUP, GROUP), GROUP)

    def y_copy(d):
        return send(yb.at[d], yr.at[d], ys.at[d], yrs.at[d], device(dy=d))

    for d in rs_order:
        b = block_at(d)
        for i in range(3):
            x_copy(i, d).wait_recv()
        yb[d] = half[b, my_x] + xr[0, b] + xr[1, b] + xr[2, b]
        if d:
            start(y_copy(d))
    total = yb[0]
    for d in (1, 7, 2, 6, 3, 5, 4):
        y_copy(d).wait_recv()
        total = total + yr[d]

    def z_copy(ref, send_sem, recv_sem, o):
        return send(ref.at[z], ref.at[z], send_sem.at[o], recv_sem.at[o], device(dz=o))

    def z_wait(ref, send_sem, recv_sem, o):
        at = ref.at[lax.rem(z + NZ - o, NZ)]
        send(at, at, send_sem.at[o], recv_sem.at[o], device(dz=o)).wait_recv()

    def z_sum(ref):
        value = ref[0]
        for i in range(1, NZ):
            value = value + ref[i]
        return value

    zr[z] = total
    for o in Z_FAR:
        start(z_copy(zr, zs, zrs, o))
    drain(len(sent) - len(Z_FAR))
    for o in reversed(Z_FAR):
        z_wait(zr, zs, zrs, o)
    left[y, mine] = z_sum(zr)

    def ay_copy(d, at):
        ref = left.at[at, mine]
        return send(ref, ref, ays.at[d], ayr.at[d], device(dy=d))

    def ax_copy(i, d):
        ref = left.at[block_at(-d), mine]
        return send(ref, ref, axs.at[i, d], axr.at[i, d], device(dx=X_FAR[i]))

    def ax_wait(i, d):
        ref = left.at[block_at(-d), group_rows(-X_FAR[i], 0)]
        send(ref, ref, axs.at[i, d], axr.at[i, d], device(dx=X_FAR[i])).wait_recv()

    def ac_copy(d):
        ref = left.at[block_at(-d), my_half]
        return send(ref, ref, acs.at[d], acr.at[d], sibling)

    def ac_wait(d):
        ref = left.at[block_at(-d), its_half]
        send(ref, ref, acs.at[d], acr.at[d], sibling).wait_recv()

    def al_copy(i):
        ox, oc = XC_FAR[i]
        ref = left.at[block_at(-LAST), mine]
        return send(ref, ref, als.at[i], alr.at[i], device(dx=ox, dc=oc))

    def al_wait(i):
        ox, oc = XC_FAR[i]
        ref = left.at[block_at(-LAST), group_rows(-ox, -oc)]
        send(ref, ref, als.at[i], alr.at[i], device(dx=ox, dc=oc)).wait_recv()

    for d in Y_FAR:
        start(ay_copy(d, y))
    for d in Y_NEAR:
        if d:
            ay_copy(d, block_at(-d)).wait_recv()
        if d == LAST:
            for i in range(7):
                start(al_copy(i))
        else:
            for i in range(3):
                start(ax_copy(i, d))

    def contract(d):
        b = block_at(-d)
        if d == LAST:
            for i in range(7):
                al_wait(i)
        else:
            ac_wait(d)
        pieces = jnp.concatenate(split3(left[b]), axis=0)
        r = jnp.dot(pieces, a_v[b], preferred_element_type=F32)
        g = lax.dot_general(pieces, pieces, NT, preferred_element_type=F32)
        if d:
            racc[...] += r
            gacc[...] += g
        else:
            racc[...] = r
            gacc[...] = g

    for t, d in enumerate(Y_NEAR[:-1]):
        for i in range(3):
            ax_wait(i, d)
        start(ac_copy(d))
        if t >= 2:
            contract(Y_NEAR[t - 2])
    for d in Y_NEAR[5:]:
        contract(d)

    rpart[...] = racc[0:64] + racc[64:128] + racc[128:192]

    def r_copy(i):
        ox, oc = XC_FAR[i]
        return send(rpart.at[group_rows(ox, oc)], rr.at[i], rs.at[i], rrs.at[i], device(dx=ox, dc=oc))

    for i in range(7):
        start(r_copy(i))

    def apart(body):
        pl.when(rep >= 0)(body)

    at_row = lax.broadcasted_iota(jnp.int32, (64, 64), 0)
    at_col = lax.broadcasted_iota(jnp.int32, (64, 64), 1)
    diagonal = at_row == at_col

    def steps(first, last):
        tiles = eliminate([both_v[8 * i : 8 * i + 8] for i in range(8)], first, last)
        for i in range(first // 8, 8):
            both_v[8 * i : 8 * i + 8] = tiles[i]

    @apart
    def _():
        one = gacc[0:64, 0:64]
        cross = gacc[0:64, 64:128] + gacc[64:128, 0:64]
        small = gacc[64:128, 64:128] + gacc[0:64, 128:192] + gacc[128:192, 0:64]
        gram = one + (cross + small)
        unit = jnp.where(diagonal, 1.0, 0.0).astype(F32)
        both_v[...] = jnp.concatenate([gram, unit], axis=1)
        steps(0, 16)

    total = rpart[mine]
    for i in reversed(range(7)):
        r_copy(i).wait_recv()
        total = total + rr[i]
    zr2[z] = total
    for o in Z_FAR:
        start(z_copy(zr2, z2s, z2r, o))

    @apart
    def _():
        steps(16, 64)
        both = both_v[...]
        scale = jnp.sum(jnp.where(diagonal, both[:, 0:64], 0.0), axis=1, keepdims=True)
        w_v[...] = both[:, 64:128] * (1.0 / jnp.sqrt(scale))

    drain(len(sent) - len(Z_FAR))
    for o in reversed(Z_FAR):
        z_wait(zr2, z2s, z2r, o)
    rt[mine] = z_sum(zr2)

    def q_copy(i):
        ox, oc = XC_FAR[i]
        ref = rt.at[mine]
        return send(ref, ref, qs.at[i], qr.at[i], device(dx=ox, dc=oc))

    def q_wait(i):
        ox, oc = XC_FAR[i]
        ref = rt.at[group_rows(-ox, -oc)]
        send(ref, ref, qs.at[i], qr.at[i], device(dx=ox, dc=oc)).wait_recv()

    for i in range(7):
        start(q_copy(i))

    @apart
    def _():
        for b in range(NY):
            basis_t = jnp.dot(
                w_v[...], left[b], precision=lax.Precision.HIGHEST, preferred_element_type=F32
            )
            high = basis_t.astype(BF16).astype(F32)
            low = basis_t - high
            packed = jnp.concatenate([high, high, low, low], axis=0)
            bk_ref[b * BLOCK : (b + 1) * BLOCK] = packed.T.astype(BF16)

    drain(len(sent) - len(XC_FAR))
    for i in reversed(range(7)):
        q_wait(i)
    right_t = jnp.dot(
        w_v[...], rt[...], precision=lax.Precision.HIGHEST, preferred_element_type=F32
    ) * (1.0 / REPS)
    high = right_t.astype(BF16)
    low = (right_t - high.astype(F32)).astype(BF16)
    rk_ref[...] = jnp.concatenate([high, low, high, low], axis=0)
    drain(len(sent))


def exchange(prior_t, blocks):
    dma = pltpu.SemaphoreType.DMA
    vmem = pltpu.VMEM
    return pl.pallas_call(
        exchange_kernel,
        out_shape=(
            jax.ShapeDtypeStruct((NY * BLOCK, 4 * RANK), BF16),
            jax.ShapeDtypeStruct((4 * RANK, COLS), BF16),
            jax.ShapeDtypeStruct((NY, BLOCK, COLS), BF16),
        ),
        in_specs=[pl.BlockSpec(memory_space=pltpu.HBM)] * 2,
        out_specs=(pl.BlockSpec(memory_space=pltpu.VMEM),) * 3,
        scratch_shapes=[
            vmem((RANK, BLOCK), BF16),
            vmem((NY, RANK, BLOCK), F32),
            vmem((NY, HALF, BLOCK), F32),
            vmem((NY, HALF, BLOCK), F32),
            vmem((3, NY, GROUP, BLOCK), F32),
            vmem((NY, GROUP, BLOCK), F32),
            vmem((NY, GROUP, BLOCK), F32),
            vmem((NZ, GROUP, BLOCK), F32),
            vmem((NY, RANK, BLOCK), F32),
            vmem((3 * RANK, COLS), F32),
            vmem((3 * RANK, 3 * RANK), F32),
            vmem((RANK, COLS), F32),
            vmem((7, GROUP, COLS), F32),
            vmem((NZ, GROUP, COLS), F32),
            vmem((RANK, COLS), F32),
            vmem((RANK, 2 * RANK), F32),
            vmem((RANK, RANK), F32),
            dma, dma((8,)), dma((8,)), dma((8,)),
            dma((3, 8)), dma((3, 8)),
            dma((8,)), dma((8,)),
            dma((12,)), dma((12,)),
            dma((8,)), dma((8,)),
            dma((3, 8)), dma((3, 8)),
            dma((7,)), dma((7,)),
            dma((8,)), dma((8,)),
            dma((7,)), dma((7,)),
            dma((12,)), dma((12,)),
            dma((7,)), dma((7,)),
        ],
        compiler_params=pltpu.CompilerParams(
            collective_id=0, has_side_effects=True, vmem_limit_bytes=EXCHANGE_VMEM
        ),
        name="exchange",
    )(prior_t, blocks)


def finish_kernel(basis_ref, right_ref, a_ref, update_ref, error_ref, up, er, up_sem, er_sem):
    copies = []
    for b in range(NY):
        decoded = jnp.dot(
            basis_ref[b * BLOCK : (b + 1) * BLOCK], right_ref[...], preferred_element_type=F32
        )
        up[b] = decoded.astype(BF16)
        copies.append(pltpu.make_async_copy(up.at[b], update_ref.at[b], up_sem.at[b]))
        copies[-1].start()
        er[b] = (a_ref[b].astype(F32) - decoded).astype(BF16)
        copies.append(pltpu.make_async_copy(er.at[b], error_ref.at[b], er_sem.at[b]))
        copies[-1].start()
    for copy in copies:
        copy.wait()


def finish(basis, right, blocks):
    shape = jax.ShapeDtypeStruct(blocks.shape, BF16)
    return pl.pallas_call(
        finish_kernel,
        out_shape=(shape, shape),
        in_specs=[pl.BlockSpec(memory_space=pltpu.VMEM)] * 3,
        out_specs=(pl.BlockSpec(memory_space=pl.ANY),) * 2,
        scratch_shapes=[
            pltpu.VMEM((NY, BLOCK, COLS), BF16),
            pltpu.VMEM((NY, BLOCK, COLS), BF16),
            pltpu.SemaphoreType.DMA((NY,)),
            pltpu.SemaphoreType.DMA((NY,)),
        ],
        compiler_params=pltpu.CompilerParams(vmem_limit_bytes=16 * 2**20),
        name="finish",
    )(basis, right, blocks)


def shards(accumulated, prior_right):
    block = accumulated[0]
    basis, right, held = exchange(prior_right.T, block.reshape(NY, BLOCK, COLS))
    update, error = finish(basis, right, held)
    return update.reshape(block.shape), error.reshape(accumulated.shape)


def solution(mesh):
    placed = (P("rep", None, "shard"), P("shard", None))
    return jax.shard_map(
        shards,
        mesh=mesh,
        in_specs=placed,
        out_specs=(P(None, "shard"), P("rep", None, "shard")),
        check_vma=False,
    )
```

```python
import functools

import jax
import jax.numpy as jnp
from jax import lax
from jax.experimental import pallas as pl
from jax.experimental.pallas import tpu as pltpu
from jax.sharding import PartitionSpec as P

MESH = pl.DeviceIdType.MESH
NX, NY, NZ, NC = 4, 8, 12, 2
REPS = NX * NZ * NC
RANK = 64
GROUP = RANK // (NX * NC)
HALF = RANK // NC
BLOCK = 384
COLS = 384
X_FAR = (2, 1, 3)
Y_FAR = (4, 3, 5, 2, 6, 1, 7)
RS_ORDER = Y_FAR + (0,)
RS_GROUPS = ((0, 1), (1, 2), (3, 2), (5, 3))
AG_ORDER = (0, 1, 7, 2, 6, 3, 5, 4)
AG_GROUPS = ((0, 3), (3, 2), (5, 2), (7, 1))
AG_GROUP_OF = (0, 0, 0, 1, 1, 2, 2, 3)
Z_FAR = (6, 5, 7, 4, 8, 3, 9, 2, 10, 1, 11)
XC_FAR = ((2, 1), (2, 0), (1, 1), (3, 1), (1, 0), (3, 0), (0, 1))
EXCHANGE_VMEM = int(49.95 * 2**20)
F32, BF16 = jnp.float32, jnp.bfloat16
NT = (((1,), (1,)), ((), ()))


def split3(value):
    high = value.astype(BF16)
    rest = value - high.astype(F32)
    middle = rest.astype(BF16)
    low = (rest - middle.astype(F32)).astype(BF16)
    return high, middle, low


def eliminate(tiles, first, last):
    tiles = list(tiles)
    rows = lax.broadcasted_iota(jnp.int32, (8, 1), 0)
    for k in range(first, last):
        own, at = divmod(k, 8)
        row = tiles[own][at : at + 1, :]
        scaled = row * (1.0 / row[:, k : k + 1])
        for i in range(own, 8):
            column = tiles[i][:, k : k + 1]
            if i == own:
                column = jnp.where(rows > at, column, 0.0)
            tiles[i] = tiles[i] - column * scaled
    return tiles


def exchange_kernel(
    pt_ref, a_ref, bk_ref, rk_ref, a_v,
    pt_v, part, sib, half, xr, yb, yr, zr, left, racc, gacc, rpart, rr, zr2, rt, both_v, w_v,
    pt_sem, a_sem, cs, cr, xs, xrs, ys, yrs, zs, zrs, ays, ayr, axs, axr, acs, acr,
    rs, rrs, z2s, z2r, qs, qr,
):
    rep, y = lax.axis_index("rep"), lax.axis_index("shard")
    chip = lax.div(rep, NC)
    x, z, c = lax.div(chip, NZ), lax.rem(chip, NZ), lax.rem(rep, NC)

    @functools.cache
    def device(dx=0, dy=0, dz=0, dc=0):
        return (
            (lax.rem(x + dx, NX) * NZ + lax.rem(z + dz, NZ)) * NC + lax.rem(c + dc, NC),
            lax.rem(y + dy, NY),
        )

    ahead = [lax.rem(y + d, NY) for d in range(NY)]
    behind = [lax.rem(y + NY - d, NY) for d in range(NY)]

    def group_rows(dx, dc):
        theirs = lax.rem(c + dc, NC) * NX + lax.rem(x + dx, NX)
        return pl.ds(pl.multiple_of(theirs * GROUP, GROUP), GROUP)

    def send(src, dst, send_sem, recv_sem, where):
        return pltpu.make_async_remote_copy(
            src_ref=src, dst_ref=dst, send_sem=send_sem, recv_sem=recv_sem,
            device_id=where, device_id_type=MESH,
        )

    def apart(body):
        pl.when(rep >= 0)(body)

    barrier = pltpu.get_barrier_semaphore()
    partners = (
        [device(dz=o) for o in Z_FAR]
        + [device(dy=d) for d in Y_FAR]
        + [device(dx=ox, dc=oc) for ox, oc in XC_FAR]
    )
    for partner in partners:
        pl.semaphore_signal(barrier, inc=1, device_id=partner, device_id_type=MESH)

    pt_copy = pltpu.make_async_copy(pt_ref, pt_v, pt_sem)
    pt_copy.start()
    a_copies = []
    for k, d in enumerate(RS_ORDER):
        b = ahead[d]
        a_copies.append(pltpu.make_async_copy(a_ref.at[b], a_v.at[b], a_sem.at[k]))
        a_copies[-1].start()

    mine = group_rows(0, 0)
    my_half = pl.ds(pl.multiple_of(c * HALF, HALF), HALF)
    its_half = pl.ds(pl.multiple_of((1 - c) * HALF, HALF), HALF)
    my_x = pl.ds(pl.multiple_of(x * GROUP, GROUP), GROUP)
    sibling = device(dc=1)

    pt_copy.wait()
    for k, d in enumerate(RS_ORDER):
        a_copies[k].wait()
        part[k] = lax.dot_general(
            pt_v[...], a_v[ahead[d]], NT, preferred_element_type=F32
        )
    pl.semaphore_wait(barrier, len(partners))

    def core_copy(i):
        slots = pl.ds(*RS_GROUPS[i])
        return send(part.at[slots, its_half], sib.at[slots], cs, cr.at[i], sibling)

    for i in range(len(RS_GROUPS)):
        core_copy(i).start()
    for i, (first, count) in enumerate(RS_GROUPS):
        slots = pl.ds(first, count)
        core_copy(i).wait_recv()
        half[slots] = part[slots, my_half] + sib[slots]
        for j, o in enumerate(X_FAR):
            rows = pl.ds(pl.multiple_of(lax.rem(x + o, NX) * GROUP, GROUP), GROUP)
            send(
                half.at[slots, rows], xr.at[j, slots], xs, xrs.at[i], device(dx=o)
            ).start()

    def y_copy(k):
        return send(yb.at[k], yr.at[k], ys, yrs, device(dy=RS_ORDER[k]))

    for i, (first, count) in enumerate(RS_GROUPS):
        slots = pl.ds(first, count)
        arrived = xr.at[:, slots]
        send(arrived, arrived, xs, xrs.at[i], sibling).wait_recv()
        for k in range(first, first + count):
            yb[k] = half[k, my_x] + xr[0, k] + xr[1, k] + xr[2, k]
            if k < 7:
                y_copy(k).start()
    send(yr, yr, ys, yrs, sibling).wait_recv()
    total = yb[7]
    for k in range(7):
        total = total + yr[k]

    def z_start(ref, send_sem, recv_sem):
        for o in Z_FAR:
            send(ref.at[z], ref.at[z], send_sem, recv_sem, device(dz=o)).start()

    def z_all(ref, send_sem, recv_sem):
        others = ref.at[pl.ds(0, NZ - 1)]
        return send(others, others, send_sem, recv_sem, sibling)

    def z_sum(ref):
        value = ref[0]
        for i in range(1, NZ):
            value = value + ref[i]
        return value

    zr[z] = total
    z_start(zr, zs, zrs)
    send(part.at[:, its_half], sib, cs, cr.at[0], sibling).wait_send()
    send(xr, xr, xs, xrs.at[0], sibling).wait_send()
    send(yr, yr, ys, yrs, sibling).wait_send()
    z_all(zr, zs, zrs).wait_recv()
    left[0, mine] = z_sum(zr)

    own = left.at[0, mine]
    for d in Y_FAR:
        at = AG_ORDER.index(d)
        group = AG_GROUP_OF[at]
        send(own, left.at[at, mine], ays, ayr.at[group], device(dy=d)).start()
    for i, (first, count) in enumerate(AG_GROUPS):
        slots = pl.ds(first, count)
        arrived = left.at[pl.ds(max(first, 1), count - (first == 0)), mine]
        send(arrived, arrived, ays, ayr.at[i], sibling).wait_recv()
        ref = left.at[slots, mine]
        for o in X_FAR:
            send(ref, ref, axs, axr.at[i], device(dx=o)).start()

    def core_gather(i):
        ref = left.at[pl.ds(*AG_GROUPS[i]), my_half]
        return send(ref, ref, acs, acr.at[i], sibling)

    def contract(i):
        core_gather(i).wait_recv()

        @apart
        def _():
            for k in range(AG_GROUPS[i][0], sum(AG_GROUPS[i])):
                pieces = jnp.concatenate(split3(left[k]), axis=0)
                r = jnp.dot(pieces, a_v[behind[AG_ORDER[k]]], preferred_element_type=F32)
                g = lax.dot_general(pieces, pieces, NT, preferred_element_type=F32)
                if k:
                    racc[...] += r
                    gacc[...] += g
                else:
                    racc[...] = r
                    gacc[...] = g

    for i in range(len(AG_GROUPS)):
        arrived = left.at[pl.ds(*AG_GROUPS[i]), pl.ds(0, 3 * GROUP)]
        send(arrived, arrived, axs, axr.at[i], sibling).wait_recv()
        core_gather(i).start()
        if i:
            contract(i - 1)
    contract(len(AG_GROUPS) - 1)

    rpart[...] = racc[0:64] + racc[64:128] + racc[128:192]
    for i, (ox, oc) in enumerate(XC_FAR):
        send(
            rpart.at[group_rows(ox, oc)], rr.at[i], rs, rrs, device(dx=ox, dc=oc)
        ).start()

    at_row = lax.broadcasted_iota(jnp.int32, (64, 64), 0)
    at_col = lax.broadcasted_iota(jnp.int32, (64, 64), 1)
    diagonal = at_row == at_col

    def steps(first, last):
        tiles = eliminate([both_v[8 * i : 8 * i + 8] for i in range(8)], first, last)
        for i in range(first // 8, 8):
            both_v[8 * i : 8 * i + 8] = tiles[i]

    @apart
    def _():
        one = gacc[0:64, 0:64]
        cross = gacc[0:64, 64:128] + gacc[64:128, 0:64]
        small = gacc[64:128, 64:128] + gacc[0:64, 128:192] + gacc[128:192, 0:64]
        gram = one + (cross + small)
        unit = jnp.where(diagonal, 1.0, 0.0).astype(F32)
        both_v[...] = jnp.concatenate([gram, unit], axis=1)
        steps(0, 16)

    send(rr, rr, rs, rrs, sibling).wait_recv()
    total = rpart[mine]
    for i in range(7):
        total = total + rr[i]
    zr2[z] = total
    z_start(zr2, z2s, z2r)

    @apart
    def _():
        steps(16, 64)
        both = both_v[...]
        scale = jnp.sum(jnp.where(diagonal, both[:, 0:64], 0.0), axis=1, keepdims=True)
        w_v[...] = both[:, 64:128] * (1.0 / jnp.sqrt(scale))

    z_all(zr, zs, zrs).wait_send()
    sent = left.at[pl.ds(0, 7), mine]
    send(sent, sent, ays, ayr.at[0], sibling).wait_send()
    sent = left.at[:, pl.ds(0, 3 * GROUP)]
    send(sent, sent, axs, axr.at[0], sibling).wait_send()
    sent = left.at[:, my_half]
    send(sent, sent, acs, acr.at[0], sibling).wait_send()
    send(rr, rr, rs, rrs, sibling).wait_send()
    z_all(zr2, z2s, z2r).wait_recv()
    rt[mine] = z_sum(zr2)

    ref = rt.at[mine]
    for ox, oc in XC_FAR:
        send(ref, ref, qs, qr, device(dx=ox, dc=oc)).start()

    @apart
    def _():
        for k, d in enumerate(AG_ORDER):
            basis_t = jnp.dot(
                w_v[...], left[k], precision=lax.Precision.HIGHEST, preferred_element_type=F32
            )
            high = basis_t.astype(BF16).astype(F32)
            low = basis_t - high
            packed = jnp.concatenate([high, high, low, low], axis=0)
            bk_ref[behind[d]] = packed.T.astype(BF16)

    z_all(zr2, z2s, z2r).wait_send()
    others = rt.at[pl.ds(0, RANK - GROUP)]
    send(others, others, qs, qr, sibling).wait()
    right_t = jnp.dot(
        w_v[...], rt[...], precision=lax.Precision.HIGHEST, preferred_element_type=F32
    ) * (1.0 / REPS)
    high = right_t.astype(BF16)
    low = (right_t - high.astype(F32)).astype(BF16)
    rk_ref[...] = jnp.concatenate([high, low, high, low], axis=0)


def exchange(prior_t, blocks):
    dma = pltpu.SemaphoreType.DMA
    vmem = pltpu.VMEM
    return pl.pallas_call(
        exchange_kernel,
        out_shape=(
            jax.ShapeDtypeStruct((NY, BLOCK, 4 * RANK), BF16),
            jax.ShapeDtypeStruct((4 * RANK, COLS), BF16),
            jax.ShapeDtypeStruct((NY, BLOCK, COLS), BF16),
        ),
        in_specs=[pl.BlockSpec(memory_space=pltpu.HBM)] * 2,
        out_specs=(pl.BlockSpec(memory_space=pltpu.VMEM),) * 3,
        scratch_shapes=[
            vmem((RANK, BLOCK), BF16),
            vmem((NY, RANK, BLOCK), F32),
            vmem((NY, HALF, BLOCK), F32),
            vmem((NY, HALF, BLOCK), F32),
            vmem((3, NY, GROUP, BLOCK), F32),
            vmem((NY, GROUP, BLOCK), F32),
            vmem((NY - 1, GROUP, BLOCK), F32),
            vmem((NZ, GROUP, BLOCK), F32),
            vmem((NY, RANK, BLOCK), F32),
            vmem((3 * RANK, COLS), F32),
            vmem((3 * RANK, 3 * RANK), F32),
            vmem((RANK, COLS), F32),
            vmem((7, GROUP, COLS), F32),
            vmem((NZ, GROUP, COLS), F32),
            vmem((RANK, COLS), F32),
            vmem((RANK, 2 * RANK), F32),
            vmem((RANK, RANK), F32),
            dma, dma((8,)), dma, dma((4,)),
            dma, dma((4,)),
            dma, dma, dma, dma,
            dma, dma((4,)),
            dma, dma((4,)),
            dma, dma((4,)),
            dma, dma, dma, dma, dma, dma,
        ],
        compiler_params=pltpu.CompilerParams(
            collective_id=0, has_side_effects=True, vmem_limit_bytes=EXCHANGE_VMEM
        ),
        name="exchange",
    )(prior_t, blocks)


def finish_kernel(basis_ref, right_ref, a_ref, update_ref, error_ref, up, er, up_sem, er_sem):
    copies = []
    for b in range(NY):
        decoded = jnp.dot(basis_ref[b], right_ref[...], preferred_element_type=F32)
        up[b] = decoded.astype(BF16)
        copies.append(pltpu.make_async_copy(up.at[b], update_ref.at[b], up_sem.at[b]))
        copies[-1].start()
        er[b] = (a_ref[b].astype(F32) - decoded).astype(BF16)
        copies.append(pltpu.make_async_copy(er.at[b], error_ref.at[b], er_sem.at[b]))
        copies[-1].start()
    for copy in copies:
        copy.wait()


def finish(basis, right, blocks):
    shape = jax.ShapeDtypeStruct(blocks.shape, BF16)
    return pl.pallas_call(
        finish_kernel,
        out_shape=(shape, shape),
        in_specs=[pl.BlockSpec(memory_space=pltpu.VMEM)] * 3,
        out_specs=(pl.BlockSpec(memory_space=pl.ANY),) * 2,
        scratch_shapes=[
            pltpu.VMEM((NY, BLOCK, COLS), BF16),
            pltpu.VMEM((NY, BLOCK, COLS), BF16),
            pltpu.SemaphoreType.DMA((NY,)),
            pltpu.SemaphoreType.DMA((NY,)),
        ],
        compiler_params=pltpu.CompilerParams(vmem_limit_bytes=16 * 2**20),
        name="finish",
    )(basis, right, blocks)


def shards(accumulated, prior_right):
    block = accumulated[0]
    basis, right, held = exchange(prior_right.T, block.reshape(NY, BLOCK, COLS))
    update, error = finish(basis, right, held)
    return update.reshape(block.shape), error.reshape(accumulated.shape)


def solution(mesh):
    placed = (P("rep", None, "shard"), P("shard", None))
    return jax.shard_map(
        shards,
        mesh=mesh,
        in_specs=placed,
        out_specs=(P(None, "shard"), P("rep", None, "shard")),
        check_vma=False,
    )
```

```python
import functools

import jax
import jax.numpy as jnp
from jax import lax
from jax.experimental import pallas as pl
from jax.experimental.pallas import tpu as pltpu
from jax.sharding import PartitionSpec as P

MESH = pl.DeviceIdType.MESH
NX, NY, NZ, NC = 4, 8, 12, 2
REPS = NX * NZ * NC
RANK = 64
GROUP = RANK // (NX * NC)
HALF = RANK // NC
BLOCK = 384
COLS = 384
X_FAR = (2, 1, 3)
Y_FAR = (4, 3, 5, 2, 6, 1, 7)
RS_ORDER = Y_FAR + (0,)
RS_GROUPS = ((0, 1), (1, 2), (3, 2), (5, 3))
AG_ORDER = (0, 1, 7, 2, 6, 3, 5, 4)
AG_GROUPS = ((0, 3), (3, 2), (5, 3))
AG_GROUP_OF = (0, 0, 0, 1, 1, 2, 2, 2)
Z_FAR = (6, 5, 7, 4, 8, 3, 9, 2, 10, 1, 11)
XC_FAR = ((2, 1), (2, 0), (1, 1), (3, 1), (1, 0), (3, 0), (0, 1))
EXCHANGE_VMEM = int(49.95 * 2**20)
F32, BF16 = jnp.float32, jnp.bfloat16
NT = (((1,), (1,)), ((), ()))


def split3(value):
    high = value.astype(BF16)
    rest = value - high.astype(F32)
    middle = rest.astype(BF16)
    low = (rest - middle.astype(F32)).astype(BF16)
    return high, middle, low


def eliminate(tiles, first, last):
    tiles = list(tiles)
    rows = lax.broadcasted_iota(jnp.int32, (8, 1), 0)
    for k in range(first, last):
        own, at = divmod(k, 8)
        row = tiles[own][at : at + 1, :]
        scaled = row * (1.0 / row[:, k : k + 1])
        for i in range(own, 8):
            column = tiles[i][:, k : k + 1]
            if i == own:
                column = jnp.where(rows > at, column, 0.0)
            tiles[i] = tiles[i] - column * scaled
    return tiles


def exchange_kernel(
    pt_ref, a_ref, bk_ref, rk_ref, a_v,
    pt_v, part, sib, half, xr, yb, yr, zr, left, pieces_v, racc, gacc, rpart, rr, zr2, rt, both_v, w_v,
    pt_sem, a_sem, cs, cr, xs, xrs, ys, yrs, zs, zrs, ays, ayr, axs, axr, acs, acr,
    rs, rrs, z2s, z2r, qs, qr,
):
    rep, y = lax.axis_index("rep"), lax.axis_index("shard")
    chip = lax.div(rep, NC)
    x, z, c = lax.div(chip, NZ), lax.rem(chip, NZ), lax.rem(rep, NC)

    @functools.cache
    def device(dx=0, dy=0, dz=0, dc=0):
        return (
            (lax.rem(x + dx, NX) * NZ + lax.rem(z + dz, NZ)) * NC + lax.rem(c + dc, NC),
            lax.rem(y + dy, NY),
        )

    ahead = [lax.rem(y + d, NY) for d in range(NY)]
    behind = [lax.rem(y + NY - d, NY) for d in range(NY)]

    def group_rows(dx, dc):
        theirs = lax.rem(c + dc, NC) * NX + lax.rem(x + dx, NX)
        return pl.ds(pl.multiple_of(theirs * GROUP, GROUP), GROUP)

    def send(src, dst, send_sem, recv_sem, where):
        return pltpu.make_async_remote_copy(
            src_ref=src, dst_ref=dst, send_sem=send_sem, recv_sem=recv_sem,
            device_id=where, device_id_type=MESH,
        )

    def apart(body):
        pl.when(rep >= 0)(body)

    barrier = pltpu.get_barrier_semaphore()
    partners = (
        [device(dz=o) for o in Z_FAR]
        + [device(dy=d) for d in Y_FAR]
        + [device(dx=ox, dc=oc) for ox, oc in XC_FAR]
    )
    for partner in partners:
        pl.semaphore_signal(barrier, inc=1, device_id=partner, device_id_type=MESH)

    pt_copy = pltpu.make_async_copy(pt_ref, pt_v, pt_sem)
    pt_copy.start()
    a_copies = []
    for k, d in enumerate(RS_ORDER):
        b = ahead[d]
        a_copies.append(pltpu.make_async_copy(a_ref.at[b], a_v.at[b], a_sem.at[k]))
        a_copies[-1].start()

    mine = group_rows(0, 0)
    my_half = pl.ds(pl.multiple_of(c * HALF, HALF), HALF)
    its_half = pl.ds(pl.multiple_of((1 - c) * HALF, HALF), HALF)
    my_x = pl.ds(pl.multiple_of(x * GROUP, GROUP), GROUP)
    sibling = device(dc=1)

    pt_copy.wait()
    for k, d in enumerate(RS_ORDER):
        a_copies[k].wait()
        part[k] = lax.dot_general(
            pt_v[...], a_v[ahead[d]], NT, preferred_element_type=F32
        )
    pl.semaphore_wait(barrier, len(partners))

    def core_copy(i):
        slots = pl.ds(*RS_GROUPS[i])
        return send(part.at[slots, its_half], sib.at[slots], cs, cr.at[i], sibling)

    for i in range(len(RS_GROUPS)):
        core_copy(i).start()
    for i, (first, count) in enumerate(RS_GROUPS):
        slots = pl.ds(first, count)
        core_copy(i).wait_recv()
        half[slots] = part[slots, my_half] + sib[slots]
        for j, o in enumerate(X_FAR):
            rows = pl.ds(pl.multiple_of(lax.rem(x + o, NX) * GROUP, GROUP), GROUP)
            send(
                half.at[slots, rows], xr.at[j, slots], xs, xrs.at[i], device(dx=o)
            ).start()

    def y_copy(k):
        return send(yb.at[k], yr.at[k], ys, yrs, device(dy=RS_ORDER[k]))

    for i, (first, count) in enumerate(RS_GROUPS):
        slots = pl.ds(first, count)
        arrived = xr.at[:, slots]
        send(arrived, arrived, xs, xrs.at[i], sibling).wait_recv()
        for k in range(first, first + count):
            yb[k] = half[k, my_x] + xr[0, k] + xr[1, k] + xr[2, k]
            if k < 7:
                y_copy(k).start()
    send(yr, yr, ys, yrs, sibling).wait_recv()
    total = yb[7]
    for k in range(7):
        total = total + yr[k]

    def z_start(ref, send_sem, recv_sem):
        for o in Z_FAR:
            send(ref.at[z], ref.at[z], send_sem, recv_sem, device(dz=o)).start()

    def z_all(ref, send_sem, recv_sem):
        others = ref.at[pl.ds(0, NZ - 1)]
        return send(others, others, send_sem, recv_sem, sibling)

    def z_sum(ref):
        value = ref[0]
        for i in range(1, NZ):
            value = value + ref[i]
        return value

    zr[z] = total
    z_start(zr, zs, zrs)
    send(part.at[:, its_half], sib, cs, cr.at[0], sibling).wait_send()
    send(xr, xr, xs, xrs.at[0], sibling).wait_send()
    send(yr, yr, ys, yrs, sibling).wait_send()
    z_all(zr, zs, zrs).wait_recv()
    left[0, mine] = z_sum(zr)

    own = left.at[0, mine]
    for d in Y_FAR:
        at = AG_ORDER.index(d)
        group = AG_GROUP_OF[at]
        send(own, left.at[at, mine], ays, ayr.at[group], device(dy=d)).start()
    for i, (first, count) in enumerate(AG_GROUPS):
        slots = pl.ds(first, count)
        arrived = left.at[pl.ds(max(first, 1), count - (first == 0)), mine]
        send(arrived, arrived, ays, ayr.at[i], sibling).wait_recv()
        ref = left.at[slots, mine]
        for o in X_FAR:
            send(ref, ref, axs, axr.at[i], device(dx=o)).start()

    def core_gather(i):
        ref = left.at[pl.ds(*AG_GROUPS[i]), my_half]
        return send(ref, ref, acs, acr.at[i], sibling)

    def contract(i):
        core_gather(i).wait_recv()

        @apart
        def _():
            for k in range(AG_GROUPS[i][0], sum(AG_GROUPS[i])):
                pieces = jnp.concatenate(split3(left[k]), axis=0)
                pieces_v[k] = pieces
                r = jnp.dot(pieces, a_v[behind[AG_ORDER[k]]], preferred_element_type=F32)
                if k:
                    racc[...] += r
                else:
                    racc[...] = r

    for i in range(len(AG_GROUPS)):
        arrived = left.at[pl.ds(*AG_GROUPS[i]), pl.ds(0, 3 * GROUP)]
        send(arrived, arrived, axs, axr.at[i], sibling).wait_recv()
        core_gather(i).start()
        if i:
            contract(i - 1)
    contract(len(AG_GROUPS) - 1)

    rpart[...] = racc[0:64] + racc[64:128] + racc[128:192]
    for i, (ox, oc) in enumerate(XC_FAR):
        send(
            rpart.at[group_rows(ox, oc)], rr.at[i], rs, rrs, device(dx=ox, dc=oc)
        ).start()

    at_row = lax.broadcasted_iota(jnp.int32, (64, 64), 0)
    at_col = lax.broadcasted_iota(jnp.int32, (64, 64), 1)
    diagonal = at_row == at_col

    def steps(first, last):
        tiles = eliminate([both_v[8 * i : 8 * i + 8] for i in range(8)], first, last)
        for i in range(first // 8, 8):
            both_v[8 * i : 8 * i + 8] = tiles[i]

    @apart
    def _():
        for k in range(NY):
            pieces = pieces_v[k]
            g = lax.dot_general(pieces, pieces, NT, preferred_element_type=F32)
            if k:
                gacc[...] += g
            else:
                gacc[...] = g
        one = gacc[0:64, 0:64]
        cross = gacc[0:64, 64:128] + gacc[64:128, 0:64]
        small = gacc[64:128, 64:128] + gacc[0:64, 128:192] + gacc[128:192, 0:64]
        gram = one + (cross + small)
        unit = jnp.where(diagonal, 1.0, 0.0).astype(F32)
        both_v[...] = jnp.concatenate([gram, unit], axis=1)
        steps(0, 12)

    send(rr, rr, rs, rrs, sibling).wait_recv()
    total = rpart[mine]
    for i in range(7):
        total = total + rr[i]
    zr2[z] = total
    z_start(zr2, z2s, z2r)

    @apart
    def _():
        steps(12, 64)
        both = both_v[...]
        scale = jnp.sum(jnp.where(diagonal, both[:, 0:64], 0.0), axis=1, keepdims=True)
        w_v[...] = both[:, 64:128] * (1.0 / jnp.sqrt(scale))

    z_all(zr, zs, zrs).wait_send()
    sent = left.at[pl.ds(0, 7), mine]
    send(sent, sent, ays, ayr.at[0], sibling).wait_send()
    sent = left.at[:, pl.ds(0, 3 * GROUP)]
    send(sent, sent, axs, axr.at[0], sibling).wait_send()
    sent = left.at[:, my_half]
    send(sent, sent, acs, acr.at[0], sibling).wait_send()
    send(rr, rr, rs, rrs, sibling).wait_send()
    z_all(zr2, z2s, z2r).wait_recv()
    rt[mine] = z_sum(zr2)

    ref = rt.at[mine]
    for ox, oc in XC_FAR:
        send(ref, ref, qs, qr, device(dx=ox, dc=oc)).start()

    @apart
    def _():
        for k, d in enumerate(AG_ORDER):
            basis_t = jnp.dot(
                w_v[...], left[k], precision=lax.Precision.HIGHEST, preferred_element_type=F32
            )
            high = basis_t.astype(BF16).astype(F32)
            low = basis_t - high
            packed = jnp.concatenate([high, high, low, low], axis=0)
            bk_ref[behind[d]] = packed.T.astype(BF16)

    z_all(zr2, z2s, z2r).wait_send()
    others = rt.at[pl.ds(0, RANK - GROUP)]
    send(others, others, qs, qr, sibling).wait()
    right_t = jnp.dot(
        w_v[...], rt[...], precision=lax.Precision.HIGHEST, preferred_element_type=F32
    ) * (1.0 / REPS)
    high = right_t.astype(BF16)
    low = (right_t - high.astype(F32)).astype(BF16)
    rk_ref[...] = jnp.concatenate([high, low, high, low], axis=0)


def exchange(prior_t, blocks):
    dma = pltpu.SemaphoreType.DMA
    vmem = pltpu.VMEM
    return pl.pallas_call(
        exchange_kernel,
        out_shape=(
            jax.ShapeDtypeStruct((NY, BLOCK, 4 * RANK), BF16),
            jax.ShapeDtypeStruct((4 * RANK, COLS), BF16),
            jax.ShapeDtypeStruct((NY, BLOCK, COLS), BF16),
        ),
        in_specs=[pl.BlockSpec(memory_space=pltpu.HBM)] * 2,
        out_specs=(pl.BlockSpec(memory_space=pltpu.VMEM),) * 3,
        scratch_shapes=[
            vmem((RANK, BLOCK), BF16),
            vmem((NY, RANK, BLOCK), F32),
            vmem((NY, HALF, BLOCK), F32),
            vmem((NY, HALF, BLOCK), F32),
            vmem((3, NY, GROUP, BLOCK), F32),
            vmem((NY, GROUP, BLOCK), F32),
            vmem((NY - 1, GROUP, BLOCK), F32),
            vmem((NZ, GROUP, BLOCK), F32),
            vmem((NY, RANK, BLOCK), F32),
            vmem((NY, 3 * RANK, BLOCK), BF16),
            vmem((3 * RANK, COLS), F32),
            vmem((3 * RANK, 3 * RANK), F32),
            vmem((RANK, COLS), F32),
            vmem((7, GROUP, COLS), F32),
            vmem((NZ, GROUP, COLS), F32),
            vmem((RANK, COLS), F32),
            vmem((RANK, 2 * RANK), F32),
            vmem((RANK, RANK), F32),
            dma, dma((8,)), dma, dma((4,)),
            dma, dma((4,)),
            dma, dma, dma, dma,
            dma, dma((4,)),
            dma, dma((4,)),
            dma, dma((4,)),
            dma, dma, dma, dma, dma, dma,
        ],
        compiler_params=pltpu.CompilerParams(
            collective_id=0, has_side_effects=True, vmem_limit_bytes=EXCHANGE_VMEM
        ),
        name="exchange",
    )(prior_t, blocks)


def finish_kernel(basis_ref, right_ref, a_ref, update_ref, error_ref, up, er, up_sem, er_sem):
    copies = []
    for b in range(NY):
        decoded = jnp.dot(basis_ref[b], right_ref[...], preferred_element_type=F32)
        up[b] = decoded.astype(BF16)
        copies.append(pltpu.make_async_copy(up.at[b], update_ref.at[b], up_sem.at[b]))
        copies[-1].start()
        er[b] = (a_ref[b].astype(F32) - decoded).astype(BF16)
        copies.append(pltpu.make_async_copy(er.at[b], error_ref.at[b], er_sem.at[b]))
        copies[-1].start()
    for copy in copies:
        copy.wait()


def finish(basis, right, blocks):
    shape = jax.ShapeDtypeStruct(blocks.shape, BF16)
    return pl.pallas_call(
        finish_kernel,
        out_shape=(shape, shape),
        in_specs=[pl.BlockSpec(memory_space=pltpu.VMEM)] * 3,
        out_specs=(pl.BlockSpec(memory_space=pl.ANY),) * 2,
        scratch_shapes=[
            pltpu.VMEM((NY, BLOCK, COLS), BF16),
            pltpu.VMEM((NY, BLOCK, COLS), BF16),
            pltpu.SemaphoreType.DMA((NY,)),
            pltpu.SemaphoreType.DMA((NY,)),
        ],
        compiler_params=pltpu.CompilerParams(vmem_limit_bytes=16 * 2**20),
        name="finish",
    )(basis, right, blocks)


def shards(accumulated, prior_right):
    block = accumulated[0]
    basis, right, held = exchange(prior_right.T, block.reshape(NY, BLOCK, COLS))
    update, error = finish(basis, right, held)
    return update.reshape(block.shape), error.reshape(accumulated.shape)


def solution(mesh):
    placed = (P("rep", None, "shard"), P("shard", None))
    return jax.shard_map(
        shards,
        mesh=mesh,
        in_specs=placed,
        out_specs=(P(None, "shard"), P("rep", None, "shard")),
        check_vma=False,
    )
```

```python
import functools

import jax
import jax.numpy as jnp
from jax import lax
from jax.experimental import pallas as pl
from jax.experimental.pallas import tpu as pltpu
from jax.sharding import PartitionSpec as P

MESH = pl.DeviceIdType.MESH
NX, NY, NZ, NC = 4, 8, 12, 2
REPS = NX * NZ * NC
RANK = 64
GROUP = RANK // (NX * NC)
HALF = RANK // NC
BLOCK = 384
COLS = 384
X_FAR = (2, 1, 3)
Y_FAR = (4, 3, 5, 2, 6, 1, 7)
RS_ORDER = Y_FAR + (0,)
RS_GROUPS = ((0, 1), (1, 2), (3, 2), (5, 3))
AG_ORDER = (0, 1, 7, 2, 6, 3, 5, 4)
AG_GROUPS = ((0, 3), (3, 2), (5, 2))
CORE_GROUPS = ((0, 3), (3, 2), (5, 3))
AG_GROUP_OF = (0, 0, 0, 1, 1, 2, 2, 3)
ACROSS = 4
Z_FAR = (6, 5, 7, 4, 8, 3, 9, 2, 10, 1, 11)
XC_FAR = ((2, 1), (2, 0), (1, 1), (3, 1), (1, 0), (3, 0), (0, 1))
EXCHANGE_VMEM = int(49.95 * 2**20)
F32, BF16 = jnp.float32, jnp.bfloat16
NT = (((1,), (1,)), ((), ()))


def split3(value):
    high = value.astype(BF16)
    rest = value - high.astype(F32)
    middle = rest.astype(BF16)
    low = (rest - middle.astype(F32)).astype(BF16)
    return high, middle, low


def eliminate(tiles, first, last):
    tiles = list(tiles)
    rows = lax.broadcasted_iota(jnp.int32, (8, 1), 0)
    for k in range(first, last):
        own, at = divmod(k, 8)
        row = tiles[own][at : at + 1, :]
        scaled = row * (1.0 / row[:, k : k + 1])
        for i in range(own, 8):
            column = tiles[i][:, k : k + 1]
            if i == own:
                column = jnp.where(rows > at, column, 0.0)
            tiles[i] = tiles[i] - column * scaled
    return tiles


def exchange_kernel(
    pt_ref, a_ref, bk_ref, rk_ref, a_v,
    pt_v, part, sib, half, xr, yb, yr, zr, left, pieces_v, racc, gacc, rpart, rr, zr2, rt, both_v, w_v,
    pt_sem, a_sem, cs, cr, xs, xrs, ys, yrs, zs, zrs, ays, ayr, axs, axr, acs, acr,
    rs, rrs, z2s, z2r, qs, qr,
):
    rep, y = lax.axis_index("rep"), lax.axis_index("shard")
    chip = lax.div(rep, NC)
    x, z, c = lax.div(chip, NZ), lax.rem(chip, NZ), lax.rem(rep, NC)

    @functools.cache
    def device(dx=0, dy=0, dz=0, dc=0):
        return (
            (lax.rem(x + dx, NX) * NZ + lax.rem(z + dz, NZ)) * NC + lax.rem(c + dc, NC),
            lax.rem(y + dy, NY),
        )

    ahead = [lax.rem(y + d, NY) for d in range(NY)]
    behind = [lax.rem(y + NY - d, NY) for d in range(NY)]

    def group_rows(dx, dc):
        theirs = lax.rem(c + dc, NC) * NX + lax.rem(x + dx, NX)
        return pl.ds(pl.multiple_of(theirs * GROUP, GROUP), GROUP)

    def send(src, dst, send_sem, recv_sem, where):
        return pltpu.make_async_remote_copy(
            src_ref=src, dst_ref=dst, send_sem=send_sem, recv_sem=recv_sem,
            device_id=where, device_id_type=MESH,
        )

    def apart(body):
        pl.when(rep >= 0)(body)

    barrier = pltpu.get_barrier_semaphore()
    partners = (
        [device(dz=o) for o in Z_FAR]
        + [device(dy=d) for d in Y_FAR]
        + [device(dx=ox, dc=oc) for ox, oc in XC_FAR]
        + [device(dx=o, dy=ACROSS) for o in X_FAR]
    )
    for partner in partners:
        pl.semaphore_signal(barrier, inc=1, device_id=partner, device_id_type=MESH)

    pt_copy = pltpu.make_async_copy(pt_ref, pt_v, pt_sem)
    pt_copy.start()
    a_copies = []
    for k, d in enumerate(RS_ORDER):
        b = ahead[d]
        a_copies.append(pltpu.make_async_copy(a_ref.at[b], a_v.at[b], a_sem.at[k]))
        a_copies[-1].start()

    mine = group_rows(0, 0)
    my_half = pl.ds(pl.multiple_of(c * HALF, HALF), HALF)
    its_half = pl.ds(pl.multiple_of((1 - c) * HALF, HALF), HALF)
    my_x = pl.ds(pl.multiple_of(x * GROUP, GROUP), GROUP)
    sibling = device(dc=1)

    pt_copy.wait()
    for k, d in enumerate(RS_ORDER):
        a_copies[k].wait()
        part[k] = lax.dot_general(
            pt_v[...], a_v[ahead[d]], NT, preferred_element_type=F32
        )
    pl.semaphore_wait(barrier, len(partners))

    def core_copy(i):
        slots = pl.ds(*RS_GROUPS[i])
        return send(part.at[slots, its_half], sib.at[slots], cs, cr.at[i], sibling)

    for i in range(len(RS_GROUPS)):
        core_copy(i).start()
    for i, (first, count) in enumerate(RS_GROUPS):
        slots = pl.ds(first, count)
        core_copy(i).wait_recv()
        half[slots] = part[slots, my_half] + sib[slots]
        if i == 0:
            send(half.at[0, my_x], yr.at[0], ys, yrs, device(dy=ACROSS)).start()
        for j, o in enumerate(X_FAR):
            rows = pl.ds(pl.multiple_of(lax.rem(x + o, NX) * GROUP, GROUP), GROUP)
            if i == 0:
                send(
                    half.at[0, rows], yr.at[7 + j], ys, yrs, device(dx=o, dy=ACROSS)
                ).start()
                continue
            send(
                half.at[slots, rows], xr.at[j, slots], xs, xrs.at[i], device(dx=o)
            ).start()

    def y_copy(k):
        return send(yb.at[k], yr.at[k], ys, yrs, device(dy=RS_ORDER[k]))

    for i, (first, count) in enumerate(RS_GROUPS):
        if i == 0:
            continue
        slots = pl.ds(first, count)
        arrived = xr.at[:, slots]
        send(arrived, arrived, xs, xrs.at[i], sibling).wait_recv()
        for k in range(first, first + count):
            yb[k] = half[k, my_x] + xr[0, k] + xr[1, k] + xr[2, k]
            if k < 7:
                y_copy(k).start()
    send(yr, yr, ys, yrs, sibling).wait_recv()
    total = yb[7]
    for k in range(10):
        total = total + yr[k]

    def z_start(ref, send_sem, recv_sem):
        for o in Z_FAR:
            send(ref.at[z], ref.at[z], send_sem, recv_sem, device(dz=o)).start()

    def z_all(ref, send_sem, recv_sem):
        others = ref.at[pl.ds(0, NZ - 1)]
        return send(others, others, send_sem, recv_sem, sibling)

    def z_sum(ref):
        value = ref[0]
        for i in range(1, NZ):
            value = value + ref[i]
        return value

    zr[z] = total
    z_start(zr, zs, zrs)
    send(part.at[:, its_half], sib, cs, cr.at[0], sibling).wait_send()
    passed = xr.at[:, pl.ds(1, NY - 1)]
    send(passed, passed, xs, xrs.at[0], sibling).wait_send()
    send(yr, yr, ys, yrs, sibling).wait_send()
    z_all(zr, zs, zrs).wait_recv()
    left[0, mine] = z_sum(zr)

    own = left.at[0, mine]
    for d in Y_FAR:
        at = AG_ORDER.index(d)
        group = AG_GROUP_OF[at]
        send(own, left.at[at, mine], ays, ayr.at[group], device(dy=d)).start()
        if d == ACROSS:
            for o in X_FAR:
                send(own, left.at[at, mine], ays, axr.at[group], device(dx=o, dy=d)).start()
    for i, (first, count) in enumerate(AG_GROUPS):
        slots = pl.ds(first, count)
        arrived = left.at[pl.ds(max(first, 1), count - (first == 0)), mine]
        send(arrived, arrived, ays, ayr.at[i], sibling).wait_recv()
        ref = left.at[slots, mine]
        for o in X_FAR:
            send(ref, ref, axs, axr.at[i], device(dx=o)).start()

    def core_gather(i):
        ref = left.at[pl.ds(*CORE_GROUPS[i]), my_half]
        return send(ref, ref, acs, acr.at[i], sibling)

    def contract(i):
        core_gather(i).wait_recv()

        @apart
        def _():
            for k in range(CORE_GROUPS[i][0], sum(CORE_GROUPS[i])):
                pieces = jnp.concatenate(split3(left[k]), axis=0)
                pieces_v[k] = pieces
                r = jnp.dot(pieces, a_v[behind[AG_ORDER[k]]], preferred_element_type=F32)
                if k:
                    racc[...] += r
                else:
                    racc[...] = r

    for i in range(len(AG_GROUPS)):
        arrived = left.at[pl.ds(*AG_GROUPS[i]), pl.ds(0, 3 * GROUP)]
        send(arrived, arrived, axs, axr.at[i], sibling).wait_recv()
        if i == len(AG_GROUPS) - 1:
            arrived = left.at[NY - 1, mine]
            send(arrived, arrived, ays, ayr.at[i + 1], sibling).wait_recv()
            arrived = left.at[NY - 1, pl.ds(0, 3 * GROUP)]
            send(arrived, arrived, ays, axr.at[i + 1], sibling).wait_recv()
        core_gather(i).start()
        if i:
            contract(i - 1)
    contract(len(AG_GROUPS) - 1)

    rpart[...] = racc[0:64] + racc[64:128] + racc[128:192]
    for i, (ox, oc) in enumerate(XC_FAR):
        send(
            rpart.at[group_rows(ox, oc)], rr.at[i], rs, rrs, device(dx=ox, dc=oc)
        ).start()

    at_row = lax.broadcasted_iota(jnp.int32, (64, 64), 0)
    at_col = lax.broadcasted_iota(jnp.int32, (64, 64), 1)
    diagonal = at_row == at_col

    def steps(first, last):
        tiles = eliminate([both_v[8 * i : 8 * i + 8] for i in range(8)], first, last)
        for i in range(first // 8, 8):
            both_v[8 * i : 8 * i + 8] = tiles[i]

    @apart
    def _():
        for k in range(NY):
            pieces = pieces_v[k]
            g = lax.dot_general(pieces, pieces, NT, preferred_element_type=F32)
            if k:
                gacc[...] += g
            else:
                gacc[...] = g
        one = gacc[0:64, 0:64]
        cross = gacc[0:64, 64:128] + gacc[64:128, 0:64]
        small = gacc[64:128, 64:128] + gacc[0:64, 128:192] + gacc[128:192, 0:64]
        gram = one + (cross + small)
        unit = jnp.where(diagonal, 1.0, 0.0).astype(F32)
        both_v[...] = jnp.concatenate([gram, unit], axis=1)
        steps(0, 12)

    send(rr, rr, rs, rrs, sibling).wait_recv()
    total = rpart[mine]
    for i in range(7):
        total = total + rr[i]
    zr2[z] = total
    z_start(zr2, z2s, z2r)

    @apart
    def _():
        steps(12, 64)
        both = both_v[...]
        scale = jnp.sum(jnp.where(diagonal, both[:, 0:64], 0.0), axis=1, keepdims=True)
        w_v[...] = both[:, 64:128] * (1.0 / jnp.sqrt(scale))

    z_all(zr, zs, zrs).wait_send()
    send(yr, yr, ays, ayr.at[0], sibling).wait_send()
    sent = left.at[pl.ds(0, 7), pl.ds(0, 3 * GROUP)]
    send(sent, sent, axs, axr.at[0], sibling).wait_send()
    sent = left.at[:, my_half]
    send(sent, sent, acs, acr.at[0], sibling).wait_send()
    send(rr, rr, rs, rrs, sibling).wait_send()
    z_all(zr2, z2s, z2r).wait_recv()
    rt[mine] = z_sum(zr2)

    ref = rt.at[mine]
    for ox, oc in XC_FAR:
        send(ref, ref, qs, qr, device(dx=ox, dc=oc)).start()

    @apart
    def _():
        for k, d in enumerate(AG_ORDER):
            basis_t = jnp.dot(
                w_v[...], left[k], precision=lax.Precision.HIGHEST, preferred_element_type=F32
            )
            high = basis_t.astype(BF16).astype(F32)
            low = basis_t - high
            packed = jnp.concatenate([high, high, low, low], axis=0)
            bk_ref[behind[d]] = packed.T.astype(BF16)

    z_all(zr2, z2s, z2r).wait_send()
    others = rt.at[pl.ds(0, RANK - GROUP)]
    send(others, others, qs, qr, sibling).wait()
    right_t = jnp.dot(
        w_v[...], rt[...], precision=lax.Precision.HIGHEST, preferred_element_type=F32
    ) * (1.0 / REPS)
    high = right_t.astype(BF16)
    low = (right_t - high.astype(F32)).astype(BF16)
    rk_ref[...] = jnp.concatenate([high, low, high, low], axis=0)


def exchange(prior_t, blocks):
    dma = pltpu.SemaphoreType.DMA
    vmem = pltpu.VMEM
    return pl.pallas_call(
        exchange_kernel,
        out_shape=(
            jax.ShapeDtypeStruct((NY, BLOCK, 4 * RANK), BF16),
            jax.ShapeDtypeStruct((4 * RANK, COLS), BF16),
            jax.ShapeDtypeStruct((NY, BLOCK, COLS), BF16),
        ),
        in_specs=[pl.BlockSpec(memory_space=pltpu.HBM)] * 2,
        out_specs=(pl.BlockSpec(memory_space=pltpu.VMEM),) * 3,
        scratch_shapes=[
            vmem((RANK, BLOCK), BF16),
            vmem((NY, RANK, BLOCK), F32),
            vmem((NY, HALF, BLOCK), F32),
            vmem((NY, HALF, BLOCK), F32),
            vmem((3, NY, GROUP, BLOCK), F32),
            vmem((NY, GROUP, BLOCK), F32),
            vmem((NY + 2, GROUP, BLOCK), F32),
            vmem((NZ, GROUP, BLOCK), F32),
            vmem((NY, RANK, BLOCK), F32),
            vmem((NY, 3 * RANK, BLOCK), BF16),
            vmem((3 * RANK, COLS), F32),
            vmem((3 * RANK, 3 * RANK), F32),
            vmem((RANK, COLS), F32),
            vmem((7, GROUP, COLS), F32),
            vmem((NZ, GROUP, COLS), F32),
            vmem((RANK, COLS), F32),
            vmem((RANK, 2 * RANK), F32),
            vmem((RANK, RANK), F32),
            dma, dma((8,)), dma, dma((4,)),
            dma, dma((4,)),
            dma, dma, dma, dma,
            dma, dma((4,)),
            dma, dma((4,)),
            dma, dma((4,)),
            dma, dma, dma, dma, dma, dma,
        ],
        compiler_params=pltpu.CompilerParams(
            collective_id=0, has_side_effects=True, vmem_limit_bytes=EXCHANGE_VMEM
        ),
        name="exchange",
    )(prior_t, blocks)


def finish_kernel(basis_ref, right_ref, a_ref, update_ref, error_ref, up, er, up_sem, er_sem):
    copies = []
    for b in range(NY):
        decoded = jnp.dot(basis_ref[b], right_ref[...], preferred_element_type=F32)
        up[b] = decoded.astype(BF16)
        copies.append(pltpu.make_async_copy(up.at[b], update_ref.at[b], up_sem.at[b]))
        copies[-1].start()
        er[b] = (a_ref[b].astype(F32) - decoded).astype(BF16)
        copies.append(pltpu.make_async_copy(er.at[b], error_ref.at[b], er_sem.at[b]))
        copies[-1].start()
    for copy in copies:
        copy.wait()


def finish(basis, right, blocks):
    shape = jax.ShapeDtypeStruct(blocks.shape, BF16)
    return pl.pallas_call(
        finish_kernel,
        out_shape=(shape, shape),
        in_specs=[pl.BlockSpec(memory_space=pltpu.VMEM)] * 3,
        out_specs=(pl.BlockSpec(memory_space=pl.ANY),) * 2,
        scratch_shapes=[
            pltpu.VMEM((NY, BLOCK, COLS), BF16),
            pltpu.VMEM((NY, BLOCK, COLS), BF16),
            pltpu.SemaphoreType.DMA((NY,)),
            pltpu.SemaphoreType.DMA((NY,)),
        ],
        compiler_params=pltpu.CompilerParams(vmem_limit_bytes=16 * 2**20),
        name="finish",
    )(basis, right, blocks)


def shards(accumulated, prior_right):
    block = accumulated[0]
    basis, right, held = exchange(prior_right.T, block.reshape(NY, BLOCK, COLS))
    update, error = finish(basis, right, held)
    return update.reshape(block.shape), error.reshape(accumulated.shape)


def solution(mesh):
    placed = (P("rep", None, "shard"), P("shard", None))
    return jax.shard_map(
        shards,
        mesh=mesh,
        in_specs=placed,
        out_specs=(P(None, "shard"), P("rep", None, "shard")),
        check_vma=False,
    )
```

```python
import functools

import jax
import jax.numpy as jnp
from jax import lax
from jax.experimental import pallas as pl
from jax.experimental.pallas import tpu as pltpu
from jax.sharding import PartitionSpec as P

MESH = pl.DeviceIdType.MESH
NX, NY, NZ, NC = 4, 8, 12, 2
REPS = NX * NZ * NC
RANK = 64
GROUP = RANK // (NX * NC)
HALF = RANK // NC
BLOCK = 384
COLS = 384
X_FAR = (2, 1, 3)
Y_FAR = (4, 3, 5, 2, 6, 1, 7)
RS_ORDER = Y_FAR + (0,)
RS_GROUPS = ((0, 1), (1, 2), (3, 2), (5, 3))
AG_ORDER = (0, 1, 7, 2, 6, 3, 5, 4)
AG_GROUPS = ((0, 3), (3, 2), (5, 3))
AG_GROUP_OF = (0, 0, 0, 1, 1, 2, 2, 2)
Z_FAR = (6, 5, 7, 4, 8, 3, 9, 2, 10, 1, 11)
XC_FAR = ((2, 1), (2, 0), (1, 1), (3, 1), (1, 0), (3, 0), (0, 1))
EXCHANGE_VMEM = int(49.95 * 2**20)
F32, BF16 = jnp.float32, jnp.bfloat16
NT = (((1,), (1,)), ((), ()))


def split3(value):
    high = value.astype(BF16)
    rest = value - high.astype(F32)
    middle = rest.astype(BF16)
    low = (rest - middle.astype(F32)).astype(BF16)
    return high, middle, low


def eliminate(tiles, first, last):
    tiles = list(tiles)
    rows = lax.broadcasted_iota(jnp.int32, (8, 1), 0)
    for k in range(first, last):
        own, at = divmod(k, 8)
        row = tiles[own][at : at + 1, :]
        scaled = row * (1.0 / row[:, k : k + 1])
        for i in range(own, 8):
            column = tiles[i][:, k : k + 1]
            if i == own:
                column = jnp.where(rows > at, column, 0.0)
            tiles[i] = tiles[i] - column * scaled
    return tiles


def exchange_kernel(
    pt_ref, a_ref, bk_ref, rk_ref, a_v,
    part, sib, half, xr, yb, yr, zr, left, pieces_v, racc, gacc, rpart, rr, zr2, rt, both_v, w_v,
    a_sem, cs, cr, xs, xrs, ys, yrs, zs, zrs, ays, ayr, axs, axr, acs, acr,
    rs, rrs, z2s, z2r, qs, qr,
):
    rep, y = lax.axis_index("rep"), lax.axis_index("shard")
    chip = lax.div(rep, NC)
    x, z, c = lax.div(chip, NZ), lax.rem(chip, NZ), lax.rem(rep, NC)

    @functools.cache
    def device(dx=0, dy=0, dz=0, dc=0):
        return (
            (lax.rem(x + dx, NX) * NZ + lax.rem(z + dz, NZ)) * NC + lax.rem(c + dc, NC),
            lax.rem(y + dy, NY),
        )

    ahead = [lax.rem(y + d, NY) for d in range(NY)]
    behind = [lax.rem(y + NY - d, NY) for d in range(NY)]

    def group_rows(dx, dc):
        theirs = lax.rem(c + dc, NC) * NX + lax.rem(x + dx, NX)
        return pl.ds(pl.multiple_of(theirs * GROUP, GROUP), GROUP)

    def send(src, dst, send_sem, recv_sem, where):
        return pltpu.make_async_remote_copy(
            src_ref=src, dst_ref=dst, send_sem=send_sem, recv_sem=recv_sem,
            device_id=where, device_id_type=MESH,
        )

    def apart(body):
        pl.when(rep >= 0)(body)

    barrier = pltpu.get_barrier_semaphore()
    partners = (
        [device(dz=o) for o in Z_FAR]
        + [device(dy=d) for d in Y_FAR]
        + [device(dx=ox, dc=oc) for ox, oc in XC_FAR]
    )
    for partner in partners:
        pl.semaphore_signal(barrier, inc=1, device_id=partner, device_id_type=MESH)

    a_copies = []
    for k, d in enumerate(RS_ORDER):
        b = ahead[d]
        a_copies.append(pltpu.make_async_copy(a_ref.at[b], a_v.at[b], a_sem.at[k]))
        a_copies[-1].start()

    mine = group_rows(0, 0)
    my_half = pl.ds(pl.multiple_of(c * HALF, HALF), HALF)
    its_half = pl.ds(pl.multiple_of((1 - c) * HALF, HALF), HALF)
    my_x = pl.ds(pl.multiple_of(x * GROUP, GROUP), GROUP)
    sibling = device(dc=1)

    for k, d in enumerate(RS_ORDER):
        a_copies[k].wait()
        part[k] = lax.dot_general(
            pt_ref[...], a_v[ahead[d]], NT, preferred_element_type=F32
        )
    pl.semaphore_wait(barrier, len(partners))

    def core_copy(i):
        slots = pl.ds(*RS_GROUPS[i])
        return send(part.at[slots, its_half], sib.at[slots], cs, cr.at[i], sibling)

    for i in range(len(RS_GROUPS)):
        core_copy(i).start()
    for i, (first, count) in enumerate(RS_GROUPS):
        slots = pl.ds(first, count)
        core_copy(i).wait_recv()
        half[slots] = part[slots, my_half] + sib[slots]
        for j, o in enumerate(X_FAR):
            rows = pl.ds(pl.multiple_of(lax.rem(x + o, NX) * GROUP, GROUP), GROUP)
            send(
                half.at[slots, rows], xr.at[j, slots], xs, xrs.at[i], device(dx=o)
            ).start()

    def y_copy(k):
        return send(yb.at[k], yr.at[k], ys, yrs, device(dy=RS_ORDER[k]))

    for i, (first, count) in enumerate(RS_GROUPS):
        slots = pl.ds(first, count)
        arrived = xr.at[:, slots]
        send(arrived, arrived, xs, xrs.at[i], sibling).wait_recv()
        for k in range(first, first + count):
            yb[k] = half[k, my_x] + xr[0, k] + xr[1, k] + xr[2, k]
            if k < 7:
                y_copy(k).start()
    send(yr, yr, ys, yrs, sibling).wait_recv()
    total = yb[7]
    for k in range(7):
        total = total + yr[k]

    def z_start(ref, send_sem, recv_sem):
        for o in Z_FAR:
            send(ref.at[z], ref.at[z], send_sem, recv_sem, device(dz=o)).start()

    def z_all(ref, send_sem, recv_sem):
        others = ref.at[pl.ds(0, NZ - 1)]
        return send(others, others, send_sem, recv_sem, sibling)

    def z_sum(ref):
        value = ref[0]
        for i in range(1, NZ):
            value = value + ref[i]
        return value

    zr[z] = total
    z_start(zr, zs, zrs)
    send(part.at[:, its_half], sib, cs, cr.at[0], sibling).wait_send()
    send(xr, xr, xs, xrs.at[0], sibling).wait_send()
    send(yr, yr, ys, yrs, sibling).wait_send()
    z_all(zr, zs, zrs).wait_recv()
    left[0, mine] = z_sum(zr)

    own = left.at[0, mine]
    for d in Y_FAR:
        at = AG_ORDER.index(d)
        group = AG_GROUP_OF[at]
        send(own, left.at[at, mine], ays, ayr.at[group], device(dy=d)).start()
    for i, (first, count) in enumerate(AG_GROUPS):
        slots = pl.ds(first, count)
        arrived = left.at[pl.ds(max(first, 1), count - (first == 0)), mine]
        send(arrived, arrived, ays, ayr.at[i], sibling).wait_recv()
        ref = left.at[slots, mine]
        for o in X_FAR:
            send(ref, ref, axs, axr.at[i], device(dx=o)).start()

    def core_gather(i):
        ref = left.at[pl.ds(*AG_GROUPS[i]), my_half]
        return send(ref, ref, acs, acr.at[i], sibling)

    def contract(i):
        core_gather(i).wait_recv()

        @apart
        def _():
            r = racc[...] if i else 0.0
            for k in range(AG_GROUPS[i][0], sum(AG_GROUPS[i])):
                pieces = jnp.concatenate(split3(left[k]), axis=0)
                pieces_v[k] = pieces
                r += jnp.dot(pieces, a_v[behind[AG_ORDER[k]]], preferred_element_type=F32)
            if i < len(AG_GROUPS) - 1:
                racc[...] = r
            else:
                rpart[...] = r[0:64] + r[64:128] + r[128:192]

    for i in range(len(AG_GROUPS)):
        arrived = left.at[pl.ds(*AG_GROUPS[i]), pl.ds(0, 3 * GROUP)]
        send(arrived, arrived, axs, axr.at[i], sibling).wait_recv()
        core_gather(i).start()
        if i:
            contract(i - 1)
    contract(len(AG_GROUPS) - 1)

    for i, (ox, oc) in enumerate(XC_FAR):
        send(
            rpart.at[group_rows(ox, oc)], rr.at[i], rs, rrs, device(dx=ox, dc=oc)
        ).start()

    at_row = lax.broadcasted_iota(jnp.int32, (64, 64), 0)
    at_col = lax.broadcasted_iota(jnp.int32, (64, 64), 1)
    diagonal = at_row == at_col

    def steps(first, last):
        tiles = eliminate([both_v[8 * i : 8 * i + 8] for i in range(8)], first, last)
        for i in range(first // 8, 8):
            both_v[8 * i : 8 * i + 8] = tiles[i]

    @apart
    def _():
        for k in range(NY):
            pieces = pieces_v[k]
            g = lax.dot_general(pieces, pieces, NT, preferred_element_type=F32)
            if k:
                gacc[...] += g
            else:
                gacc[...] = g
        one = gacc[0:64, 0:64]
        cross = gacc[0:64, 64:128] + gacc[64:128, 0:64]
        small = gacc[64:128, 64:128] + gacc[0:64, 128:192] + gacc[128:192, 0:64]
        gram = one + (cross + small)
        unit = jnp.where(diagonal, 1.0, 0.0).astype(F32)
        both_v[...] = jnp.concatenate([gram, unit], axis=1)
        steps(0, 12)

    send(rr, rr, rs, rrs, sibling).wait_recv()
    total = rpart[mine]
    for i in range(7):
        total = total + rr[i]
    zr2[z] = total
    z_start(zr2, z2s, z2r)

    @apart
    def _():
        steps(12, 64)
        both = both_v[...]
        scale = jnp.sum(jnp.where(diagonal, both[:, 0:64], 0.0), axis=1, keepdims=True)
        w_v[...] = both[:, 64:128] * (1.0 / jnp.sqrt(scale))

    z_all(zr, zs, zrs).wait_send()
    sent = left.at[pl.ds(0, 7), mine]
    send(sent, sent, ays, ayr.at[0], sibling).wait_send()
    sent = left.at[:, pl.ds(0, 3 * GROUP)]
    send(sent, sent, axs, axr.at[0], sibling).wait_send()
    sent = left.at[:, my_half]
    send(sent, sent, acs, acr.at[0], sibling).wait_send()
    send(rr, rr, rs, rrs, sibling).wait_send()
    z_all(zr2, z2s, z2r).wait_recv()
    rt[mine] = z_sum(zr2)

    ref = rt.at[mine]
    for ox, oc in XC_FAR:
        send(ref, ref, qs, qr, device(dx=ox, dc=oc)).start()

    @apart
    def _():
        for k, d in enumerate(AG_ORDER):
            basis_t = jnp.dot(
                w_v[...], left[k], precision=lax.Precision.HIGHEST, preferred_element_type=F32
            )
            high = basis_t.astype(BF16).astype(F32)
            low = basis_t - high
            packed = jnp.concatenate([high, high, low, low], axis=0)
            bk_ref[behind[d]] = packed.T.astype(BF16)

    z_all(zr2, z2s, z2r).wait_send()
    others = rt.at[pl.ds(0, RANK - GROUP)]
    send(others, others, qs, qr, sibling).wait()
    right_t = jnp.dot(
        w_v[...], rt[...], precision=lax.Precision.HIGHEST, preferred_element_type=F32
    ) * (1.0 / REPS)
    high = right_t.astype(BF16)
    low = (right_t - high.astype(F32)).astype(BF16)
    rk_ref[...] = jnp.concatenate([high, low, high, low], axis=0)


def exchange(prior_t, blocks):
    dma = pltpu.SemaphoreType.DMA
    vmem = pltpu.VMEM
    return pl.pallas_call(
        exchange_kernel,
        out_shape=(
            jax.ShapeDtypeStruct((NY, BLOCK, 4 * RANK), BF16),
            jax.ShapeDtypeStruct((4 * RANK, COLS), BF16),
            jax.ShapeDtypeStruct((NY, BLOCK, COLS), BF16),
        ),
        in_specs=[
            pl.BlockSpec(memory_space=pltpu.VMEM),
            pl.BlockSpec(memory_space=pltpu.HBM),
        ],
        out_specs=(pl.BlockSpec(memory_space=pltpu.VMEM),) * 3,
        scratch_shapes=[
            vmem((NY, RANK, BLOCK), F32),
            vmem((NY, HALF, BLOCK), F32),
            vmem((NY, HALF, BLOCK), F32),
            vmem((3, NY, GROUP, BLOCK), F32),
            vmem((NY, GROUP, BLOCK), F32),
            vmem((NY - 1, GROUP, BLOCK), F32),
            vmem((NZ, GROUP, BLOCK), F32),
            vmem((NY, RANK, BLOCK), F32),
            vmem((NY, 3 * RANK, BLOCK), BF16),
            vmem((3 * RANK, COLS), F32),
            vmem((3 * RANK, 3 * RANK), F32),
            vmem((RANK, COLS), F32),
            vmem((7, GROUP, COLS), F32),
            vmem((NZ, GROUP, COLS), F32),
            vmem((RANK, COLS), F32),
            vmem((RANK, 2 * RANK), F32),
            vmem((RANK, RANK), F32),
            dma((8,)), dma, dma((4,)),
            dma, dma((4,)),
            dma, dma, dma, dma,
            dma, dma((4,)),
            dma, dma((4,)),
            dma, dma((4,)),
            dma, dma, dma, dma, dma, dma,
        ],
        compiler_params=pltpu.CompilerParams(
            collective_id=0, has_side_effects=True, vmem_limit_bytes=EXCHANGE_VMEM
        ),
        name="exchange",
    )(prior_t, blocks)


def finish_kernel(basis_ref, right_ref, a_ref, update_ref, error_ref, up, er, up_sem, er_sem):
    copies = []
    for b in range(NY):
        decoded = jnp.dot(basis_ref[b], right_ref[...], preferred_element_type=F32)
        up[b] = decoded.astype(BF16)
        copies.append(pltpu.make_async_copy(up.at[b], update_ref.at[b], up_sem.at[b]))
        copies[-1].start()
        er[b] = (a_ref[b].astype(F32) - decoded).astype(BF16)
        copies.append(pltpu.make_async_copy(er.at[b], error_ref.at[b], er_sem.at[b]))
        copies[-1].start()
    for copy in copies:
        copy.wait()


def finish(basis, right, blocks):
    shape = jax.ShapeDtypeStruct(blocks.shape, BF16)
    return pl.pallas_call(
        finish_kernel,
        out_shape=(shape, shape),
        in_specs=[pl.BlockSpec(memory_space=pltpu.VMEM)] * 3,
        out_specs=(pl.BlockSpec(memory_space=pl.ANY),) * 2,
        scratch_shapes=[
            pltpu.VMEM((NY, BLOCK, COLS), BF16),
            pltpu.VMEM((NY, BLOCK, COLS), BF16),
            pltpu.SemaphoreType.DMA((NY,)),
            pltpu.SemaphoreType.DMA((NY,)),
        ],
        compiler_params=pltpu.CompilerParams(vmem_limit_bytes=16 * 2**20),
        name="finish",
    )(basis, right, blocks)


def shards(accumulated, prior_right):
    block = accumulated[0]
    basis, right, held = exchange(prior_right.T, block.reshape(NY, BLOCK, COLS))
    update, error = finish(basis, right, held)
    return update.reshape(block.shape), error.reshape(accumulated.shape)


def solution(mesh):
    placed = (P("rep", None, "shard"), P("shard", None))
    return jax.shard_map(
        shards,
        mesh=mesh,
        in_specs=placed,
        out_specs=(P(None, "shard"), P("rep", None, "shard")),
        check_vma=False,
    )
```
